256 devices in a mesh: section: 2 (over z_hi), ctx: 16 (over x, y), heads: 8 (over z_lo, core).
Axes of the slice: x: 4, y: 4, z: 8 (z_hi: 2, z_lo: 4; z = z_hi * 4 + z_lo), core: 2. Of those that a mesh axis runs over, the one named last changes fastest.
Arguments:
- grad_out: bfloat16 [4096, 4096], P('ctx'), may hold values from -6 to 6
- w_out: bfloat16 [2, 8192, 4096], P('section', 'heads', 'ctx'), may hold values from -0.09375 to 0.09375
- w_in: bfloat16 [2, 4096, 8192], P('section', 'ctx', 'heads'), may hold values from -0.09375 to 0.09375
- w_bc: bfloat16 [2, 4096, 2048], P('section', 'ctx', 'heads'), may hold values from -0.09375 to 0.09375
- x_act: bfloat16 [2, 4096, 8192], P('section', 'ctx', 'heads'), may hold values from -3 to 3
- bc_act: bfloat16 [2, 4096, 2048], P('section', 'ctx', 'heads'), may hold values from -0.29882812 to 0.29882812
- decay: float32 [2, 128, 4096], P('section', 'heads', 'ctx'), may hold values from -1.5 to 0, as said below
- skip_gain: float32 [2, 128], P('section', 'heads'), may hold values from 0.5 to 1.5
- state_in: float32 [2, 16, 128, 64, 128], P('section', 'ctx', 'heads'), may hold values from -0.6 to 0.6
Outputs:
- input_grad: bfloat16 [2, 4096, 4096], P('section', 'ctx', 'heads')
The draws below stay inside these ranges and needn't reach their ends.
Inputs may be any that keep to these rules, and one draw needn't show every extreme that they name: Log decay factors, all negative.
All inputs are finite; a program needn't handle non-finite values.
Results may differ from the reference program's by a relative error of at most 0.039.
Values may be sent and summed in bfloat16 or wider, within the bound.
No kernel may reach another device: no remote copies, remote signals or barrier semaphores. Data moves between devices by JAX's collectives and lax.ppermute only.
A program may use at most 128 MiB of HBM per device.

```python
import math
import jax
import jax.numpy as jnp
from jax import lax

D = 4096
P_SIZE = 64
N = 128
HEADS_DEV = 16
GROUPS = 8
TOK_DEV = 256
MIXER_LAYERS = 2
HEADS = 128
SEQUENCE_TOKENS = 4096
SHARDS = 16
N_HEADS = 8


def draw_decay(key, part):
    key = jax.random.fold_in(key, 11)
    random_subseeds = jax.random.split(key, 7)
    blocks = SEQUENCE_TOKENS // TOK_DEV
    fast_share = 0.5
    slow_base = jnp.exp(jax.random.uniform(random_subseeds[1], (MIXER_LAYERS, HEADS, 1, 1), minval=math.log(0.3), maxval=0.0))
    fast_base = jnp.exp(jax.random.uniform(random_subseeds[2], (MIXER_LAYERS, HEADS, 1, 1), minval=math.log(0.05), maxval=math.log(0.1)))
    is_fast = jax.random.uniform(random_subseeds[0], (MIXER_LAYERS, HEADS, 1, 1)) < fast_share
    block_factor = jnp.exp(jax.random.uniform(random_subseeds[3], (MIXER_LAYERS, HEADS, blocks, 1), minval=math.log(0.4), maxval=0.0))
    token_factor = jax.random.uniform(random_subseeds[4], (MIXER_LAYERS, HEADS, blocks, TOK_DEV), minval=0.5, maxval=1.0)
    slow_rate = slow_base * (math.log(10.0) / (3.0 * SEQUENCE_TOKENS))
    decay_rates = jnp.where(is_fast, fast_base, slow_rate) * block_factor * token_factor
    decay_rates = decay_rates.reshape(MIXER_LAYERS, HEADS, SEQUENCE_TOKENS)
    spike_positions = jax.random.randint(random_subseeds[5], (MIXER_LAYERS, 2), 0, SEQUENCE_TOKENS)
    retained_fraction = jax.random.uniform(random_subseeds[6], (MIXER_LAYERS, HEADS, 2), minval=0.5, maxval=0.8)
    token_positions = jnp.arange(SEQUENCE_TOKENS)
    spike_events = jnp.where(token_positions[None, None, :, None] == spike_positions[:, None, None, :], jnp.log(retained_fraction)[:, :, None, :], 0.0).sum(axis=-1)
    return (spike_events - decay_rates).astype(jnp.float32)


def block_scale(stream_key, extent, pieces, least, largest):
    def one(position, blocks):
        heights = jax.random.uniform(jax.random.fold_in(jax.random.fold_in(stream_key, 6), position), (blocks,), jnp.float32, least / len(pieces), largest / len(pieces))
        return jnp.repeat(jnp.exp(heights), extent[position] // blocks).reshape((-1,) + (1,) * (len(extent) - position - 1))

    level = one(*pieces[0])
    for cut in pieces[1:]:
        level = level * one(*cut)
    return level


def centred(rng, dims, deviation, reach, shards=(), dtype=jnp.bfloat16):
    array = deviation * jax.random.normal(rng, dims, jnp.float32)
    if shards:
        array = array * block_scale(rng, dims, shards, -0.22, 0.18)
    return jnp.clip(array, -reach, reach).astype(dtype)


def setup_inputs(seed: int = 0) -> dict:
    streams_of = jax.random.split(jax.random.key(seed), 10)
    return {
        "grad_out": centred(streams_of[0], (SEQUENCE_TOKENS, D), 1.0, 6.0, ((0, 16),)),
        "w_out": centred(streams_of[1], (MIXER_LAYERS, HEADS * P_SIZE, D), D ** -0.5, 0.09375, ((0, 2), (1, 8), (2, 16))),
        "w_in": centred(streams_of[2], (MIXER_LAYERS, D, HEADS * P_SIZE), D ** -0.5, 0.09375, ((0, 2), (1, 16), (2, 8))),
        "w_bc": centred(streams_of[3], (MIXER_LAYERS, D, GROUPS * 2 * N), D ** -0.5, 0.09375, ((0, 2), (1, 16), (2, 8))),
        "x_act": centred(streams_of[4], (MIXER_LAYERS, SEQUENCE_TOKENS, HEADS * P_SIZE), 0.5, 3.0, ((0, 2), (1, 16), (2, 8))),
        "bc_act": centred(streams_of[5], (MIXER_LAYERS, SEQUENCE_TOKENS, GROUPS * 2 * N), 0.05, 0.29882812, ((0, 2), (1, 16), (2, 8))),
        "decay": draw_decay(jax.random.fold_in(streams_of[9], 71), 0),
        "skip_gain": jnp.clip(1.0 + 0.1 * jax.random.normal(streams_of[7], (MIXER_LAYERS, HEADS), jnp.float32), 0.5, 1.5),
        "state_in": centred(streams_of[8], (MIXER_LAYERS, SHARDS, HEADS, P_SIZE, N), 0.1, 0.6, ((0, 2), (1, 16), (2, 8)), jnp.float32),
    }


def decay_table(decay_rates):
    cumulative = jnp.cumsum(decay_rates, axis=1)
    spread = cumulative[:, :, None] - cumulative[:, None, :]
    length = decay_rates.shape[1]
    lower_mask = jnp.arange(length)[:, None] >= jnp.arange(length)[None, :]
    mixer_function = jnp.where(lower_mask[None], jnp.exp(jnp.minimum(spread, 0.0)), 0.0)
    return (cumulative, mixer_function)

def block_summary(output_gradient_rows, output_projection_values, cumulative):
    length, groups, per_group, head_size = output_gradient_rows.shape
    leading = jnp.exp(cumulative).reshape(groups, per_group, length)
    entering = jnp.einsum('ght,tghp,tgn->ghpn', leading, output_gradient_rows, output_projection_values)
    totals = jnp.exp(cumulative[:, -1])
    return (totals, entering.reshape(groups * per_group, head_size, output_projection_values.shape[2]))

def block_grads(output_gradient_rows, x_vals, input_projection_values, output_projection_values, cumulative, mixer_function, entry_state, exit_grad, skip):
    length, groups, per_group, head_size = output_gradient_rows.shape
    state_size = input_projection_values.shape[2]
    leading = jnp.exp(cumulative).reshape(groups, per_group, length)
    trailing = jnp.exp(cumulative[:, -1:] - cumulative).reshape(groups, per_group, length)
    mixer_function = mixer_function.reshape(groups, per_group, length, length)
    entry = entry_state.reshape(groups, per_group, head_size, state_size)
    leaving = exit_grad.reshape(groups, per_group, head_size, state_size)
    skip = skip.reshape(groups, per_group)
    products = jnp.einsum('tghp,sghp->ghts', output_gradient_rows, x_vals)
    weighted = mixer_function * products
    grad_c = jnp.einsum('ghts,sgn->tgn', weighted, input_projection_values) + jnp.einsum('ght,tghp,ghpn->tgn', leading, output_gradient_rows, entry)
    common_region = jnp.einsum('lxp,fxp->xlf', output_projection_values, input_projection_values)
    input_gradient_rows = jnp.einsum('eaol,eol,oeav->leav', mixer_function, common_region, output_gradient_rows)
    input_gradient_rows = input_gradient_rows + jnp.einsum('ght,tgn,ghpn->tghp', trailing, input_projection_values, leaving) + skip[None, :, :, None] * output_gradient_rows
    grad_b = jnp.einsum('ghrt,rgn->tgn', weighted, output_projection_values) + jnp.einsum('ght,tghp,ghpn->tgn', trailing, x_vals, leaving)
    grad_bc = jnp.stack([grad_b, grad_c], axis=2).reshape(length, groups * 2 * state_size)
    return (input_gradient_rows.reshape(length, groups * per_group * head_size), grad_bc)

def layer_grad(upstream, w_out, w_in, w_bc, x_act, bc_act, decay, skip_gain, state_in):
    grad_ssd = jnp.dot(upstream, w_out.T, preferred_element_type=jnp.float32).astype(jnp.bfloat16)
    blocks = SEQUENCE_TOKENS // TOK_DEV
    per_group = HEADS // GROUPS
    inputs = []
    summaries = []
    for block_id in range(blocks):
        first_row = block_id * TOK_DEV
        output_gradient_rows = grad_ssd[first_row:first_row + TOK_DEV].astype(jnp.float32).reshape(TOK_DEV, GROUPS, per_group, P_SIZE)
        x_vals = x_act[first_row:first_row + TOK_DEV].astype(jnp.float32).reshape(TOK_DEV, GROUPS, per_group, P_SIZE)
        bc_vals = bc_act[first_row:first_row + TOK_DEV].astype(jnp.float32).reshape(TOK_DEV, GROUPS, 2, N)
        cumulative, mixer_function = decay_table(decay[:, first_row:first_row + TOK_DEV])
        inputs.append((output_gradient_rows, x_vals, bc_vals[:, :, 0], bc_vals[:, :, 1], cumulative, mixer_function))
        summaries.append(block_summary(output_gradient_rows, bc_vals[:, :, 1], cumulative))
    exits = [None] * blocks
    exits[blocks - 1] = jnp.zeros((HEADS, P_SIZE, N), jnp.float32)
    for block_id in range(blocks - 2, -1, -1):
        totals, entering = summaries[block_id + 1]
        exits[block_id] = entering + totals[:, None, None] * exits[block_id + 1]
    grads_x = []
    grads_bc = []
    for block_id in range(blocks):
        output_gradient_rows, x_vals, input_projection_values, output_projection_values, cumulative, mixer_function = inputs[block_id]
        input_gradient_rows, grad_bc = block_grads(output_gradient_rows, x_vals, input_projection_values, output_projection_values, cumulative, mixer_function, state_in[block_id], exits[block_id], skip_gain)
        grads_x.append(input_gradient_rows)
        grads_bc.append(grad_bc)
    input_gradient_rows = jnp.concatenate(grads_x, axis=0).astype(jnp.bfloat16)
    grad_bc = jnp.concatenate(grads_bc, axis=0).astype(jnp.bfloat16)
    head_cols = HEADS_DEV * P_SIZE
    group_cols = GROUPS // N_HEADS * 2 * N
    total = jnp.zeros((SEQUENCE_TOKENS, D), jnp.float32)
    for part_id in range(N_HEADS):
        term = jnp.dot(input_gradient_rows[:, part_id * head_cols:(part_id + 1) * head_cols], w_in[:, part_id * head_cols:(part_id + 1) * head_cols].T, preferred_element_type=jnp.float32)
        term = term + jnp.dot(grad_bc[:, part_id * group_cols:(part_id + 1) * group_cols], w_bc[:, part_id * group_cols:(part_id + 1) * group_cols].T, preferred_element_type=jnp.float32)
        total = total + lax.optimization_barrier(term.astype(jnp.bfloat16)).astype(jnp.float32)
    return (upstream.astype(jnp.float32) + total).astype(jnp.bfloat16)

def reference(grad_out, w_out, w_in, w_bc, x_act, bc_act, decay, skip_gain, state_in):
    upper = layer_grad(grad_out, w_out[1], w_in[1], w_bc[1], x_act[1], bc_act[1], decay[1], skip_gain[1], state_in[1])
    lower = layer_grad(upper, w_out[0], w_in[0], w_bc[0], x_act[0], bc_act[0], decay[0], skip_gain[0], state_in[0])
    return jnp.stack([lower, upper])
```

```python
import jax
import jax.numpy as jnp
from jax import lax
from jax.sharding import PartitionSpec as P

SIDE = 4
CORES = 2
BOTH = (0, 1)
AXES = ("section", "ctx", "heads")


def place(section, x, y, z, core):
    return (((section * SIDE + x) * SIDE + y) * SIDE + z) * CORES + core


def routed(value, move, sections):
    pairs = []
    for section in sections:
        for x in range(SIDE):
            for y in range(SIDE):
                for z in range(SIDE):
                    for core in range(CORES):
                        here = (section, x, y, z, core)
                        pairs.append((place(*here), place(*move(*here))))
    return lax.ppermute(value, AXES, pairs)


def along_x(k):
    return lambda s, x, y, z, c: (s, (x + k) % SIDE, y, z, c)


def along_y(k):
    return lambda s, x, y, z, c: (s, x, (y + k) % SIDE, z, c)


def across_z(k):
    return lambda s, x, y, z, c: (s, x, y, z ^ k, c)


def other_core(s, x, y, z, c):
    return (s, x, y, z, 1 - c)


def dot(left, right, left_dim, right_dim):
    return lax.dot_general(
        left, right, (((left_dim,), (right_dim,)), ((), ())), preferred_element_type=jnp.float32
    )


def column_block(value, index, width):
    return lax.dynamic_slice_in_dim(value, index * width, width, 1)


def decay_tables(decay_rates):
    cumulative = jnp.cumsum(decay_rates, axis=1)
    spread = cumulative[:, :, None] - cumulative[:, None, :]
    length = decay_rates.shape[1]
    lower = jnp.arange(length)[:, None] >= jnp.arange(length)[None, :]
    kernel = jnp.where(lower[None], jnp.exp(jnp.minimum(spread, 0.0)), 0.0)
    return cumulative, kernel


def local(grad_out, w_out, w_in, w_bc, x_act, bc_act, decay, skip_gain, state_in):
    bf16, f32 = jnp.bfloat16, jnp.float32
    section = lax.axis_index("section")
    ctx = lax.axis_index("ctx")
    heads_at = lax.axis_index("heads")
    x, y = ctx // SIDE, ctx % SIDE
    z, core = heads_at // CORES, heads_at % CORES
    rows, width = grad_out.shape
    block = width // SIDE
    share = block // CORES
    fine = w_out.shape[2]
    half = rows // CORES
    head_count, head_size, state_size = state_in.shape[2:]
    inner = head_count * head_size

    def first_step(k):
        return lambda s, x, y, z, c: (
            (s, x, (y + k) % SIDE, z, c) if s == 1 else (s, (x + k) % SIDE, y, z, c)
        )

    out_at = jnp.where(section == 1, y, x)
    out_block = jnp.zeros((inner, block), bf16)
    out_parts = [w_out[0]] + [routed(w_out[0], first_step(k), BOTH) for k in (1, 2, 3)]

    pieces = []
    for k in (1, 2, 3):
        piece = lax.dynamic_slice(grad_out, (half * core, block * ((x + k) % SIDE)), (half, block))
        pieces.append(routed(piece, along_x(k), (1,)))
    mine = jnp.stack(pieces)
    theirs = routed(mine, other_core, (1,))
    others = jnp.where(
        core == 0, jnp.concatenate([mine, theirs], 1), jnp.concatenate([theirs, mine], 1)
    )
    upstream = jnp.concatenate([column_block(grad_out, x, block)[None], others], 0)

    for k, part in enumerate(out_parts):
        out_block = lax.dynamic_update_slice(out_block, part, (0, fine * ((out_at - k) % SIDE)))

    back = jnp.concatenate([w_in[0], w_bc[0]], axis=1)
    back_block = jnp.zeros((SIDE, fine, back.shape[1]), bf16)
    for k in range(SIDE):
        part = back if k == 0 else routed(back, along_y(k), BOTH)
        back_block = lax.dynamic_update_slice(back_block, part[None], ((y - k) % SIDE, 0, 0))
    back_block = back_block.reshape(block, back.shape[1])

    cumulative, kernel = decay_tables(decay[0])
    leading = jnp.repeat(jnp.exp(cumulative).T, head_size, axis=1)
    trailing = jnp.repeat(jnp.exp(cumulative[:, -1:] - cumulative).T, head_size, axis=1)
    b_rows = bc_act[0][:, :state_size]
    c_rows = bc_act[0][:, state_size:]
    common = dot(c_rows, b_rows, 1, 1)
    mixed = (kernel * common[None]).astype(bf16)
    x_rows = x_act[0]
    x_heads = x_rows.reshape(rows, head_count, head_size)
    x_trailing = (x_rows.astype(f32) * trailing).astype(bf16)
    entry = state_in[0, 0].reshape(inner, state_size).astype(bf16)
    skip = jnp.repeat(skip_gain[0], head_size)[None]
    totals = lax.all_to_all(
        jnp.broadcast_to(cumulative[:, -1][:, None], (head_count, 128)), "ctx", 0, 0
    )[:, 0]
    run = jnp.cumsum(totals)
    at = jnp.arange(head_count)
    later = at[None, :] > at[:, None]
    carry = jnp.where(later, jnp.exp(jnp.minimum((run - totals)[None, :] - run[:, None], 0.0)), 0.0)

    def mixer(grad_ssd):
        grad_f32 = grad_ssd.astype(f32)
        grad_leading = (grad_f32 * leading).astype(bf16)
        entering = dot(grad_leading, c_rows, 0, 0).astype(bf16)
        arrived = lax.all_to_all(
            entering.reshape(head_count, head_size, state_size), "ctx", 0, 0
        ).reshape(head_count, head_size * state_size)
        exits = lax.dot_general(
            carry, arrived.astype(f32), (((1,), (0,)), ((), ())), precision=lax.Precision.HIGHEST
        )
        leaving = lax.all_to_all(
            exits.astype(bf16).reshape(head_count, head_size, state_size), "ctx", 0, 0
        ).reshape(inner, state_size)
        grad_heads = grad_ssd.reshape(rows, head_count, head_size)
        products = jnp.einsum(
            "thp,shp->hts", grad_heads, x_heads, preferred_element_type=f32
        )
        weighted = jnp.sum(kernel * products, axis=0).astype(bf16)
        grad_c = dot(weighted, b_rows, 1, 0) + dot(grad_leading, entry, 1, 0)
        grad_b = dot(weighted, c_rows, 0, 0) + dot(x_trailing, leaving, 1, 0)
        within = jnp.einsum(
            "hts,thp->shp", mixed, grad_heads, preferred_element_type=f32
        ).reshape(rows, inner)
        grad_x = within + trailing * dot(b_rows, leaving, 1, 1) + skip * grad_f32
        return jnp.concatenate([grad_x, grad_b, grad_c], axis=1).astype(bf16)

    def over_heads(terms, of_z, sections):
        keep = lax.dynamic_slice_in_dim(terms, share * core, share, 2)
        give = lax.dynamic_slice_in_dim(terms, share * (1 - core), share, 2)
        got = routed(give.astype(bf16), other_core, sections)
        pair = keep.astype(f32) + got.astype(f32)
        total = lax.dynamic_index_in_dim(pair, of_z(z), 0, False)
        pair = pair.astype(bf16)
        for k in (1, 2, 3):
            sent = lax.dynamic_index_in_dim(pair, of_z(z ^ k), 0, False)
            total = total + routed(sent, across_z(k), sections).astype(f32)
        return total

    partial = dot(upstream.reshape(SIDE * rows, block), out_block, 1, 1)
    partial = partial.reshape(SIDE, rows, inner)
    grad_ssd = partial[0]
    partial = partial.astype(bf16)
    for k in (1, 2, 3):
        grad_ssd = grad_ssd + routed(partial[k], along_x(-k), (1,)).astype(f32)
    grads = mixer(grad_ssd.astype(bf16))
    grads_all = jnp.stack([grads] + [routed(grads, along_x(k), (1,)) for k in (1, 2, 3)])
    terms = dot(grads_all.reshape(SIDE * rows, -1), back_block, 1, 1)
    total = over_heads(terms.reshape(SIDE, rows, block), lambda z: z, (1,))
    own = lax.dynamic_index_in_dim(upstream, z, 0, False)
    middle = (lax.dynamic_slice_in_dim(own, share * core, share, 1).astype(f32) + total).astype(bf16)

    arrived = routed(middle, lambda s, x, y, z, c: (0, (x - z) % SIDE, y, x, c), (1,))
    settled = routed(middle, lambda s, x, y, z, c: (s, (x - z) % SIDE, y, x, c), (1,))

    out_whole = [out_block] + [routed(out_block, along_y(k), (0,)) for k in (1, 2, 3)]
    back_whole = [back_block] + [routed(back_block, along_x(k), (0,)) for k in (1, 2, 3)]

    line = jnp.zeros((rows, SIDE, share), bf16)
    for k in range(SIDE):
        part = arrived if k == 0 else routed(arrived, across_z(k), (0,))
        line = lax.dynamic_update_slice(line, part[:, None], (0, z ^ k, 0))
    other = routed(line, other_core, (0,))
    lower = jnp.where(core == 0, jnp.stack([line, other], 2), jnp.stack([other, line], 2))
    lower = lower.reshape(rows, SIDE, SIDE, fine)
    grad_ssd = jnp.zeros((rows, inner), f32)
    for k in range(SIDE):
        columns = lax.dynamic_index_in_dim(lower, (y - k) % SIDE, 2, False).reshape(rows, block)
        grad_ssd = grad_ssd + dot(columns, out_whole[k], 1, 1)
    grads = mixer(grad_ssd.astype(bf16))
    terms = jnp.stack([dot(grads, back_whole[k], 1, 1) for k in range(SIDE)])
    total = over_heads(terms, lambda z: (x - z) % SIDE, (0,))
    result = (arrived.astype(f32) + total).astype(bf16)
    return jnp.where(section == 1, settled, result)[None]


def solution(mesh):
    placed = (
        P("ctx", None),
        P("section", "heads", "ctx"),
        P("section", "ctx", "heads"),
        P("section", "ctx", "heads"),
        P("section", "ctx", "heads"),
        P("section", "ctx", "heads"),
        P("section", "heads", "ctx"),
        P("section", "heads"),
        P("section", "ctx", "heads", None, None),
    )
    return jax.shard_map(
        local, mesh=mesh, in_specs=placed, out_specs=P("section", "ctx", "heads"), check_vma=False
    )
```

```python
import jax
import jax.numpy as jnp
from jax import lax
from jax.experimental import pallas as pl
from jax.experimental.pallas import tpu as pltpu
from jax.sharding import PartitionSpec as P

SIDE = 4
CORES = 2
BOTH = (0, 1)
AXES = ("section", "ctx", "heads")
VMEM = 40 * 1024 * 1024
bf16, f32 = jnp.bfloat16, jnp.float32


def place(section, x, y, z, core):
    return (((section * SIDE + x) * SIDE + y) * SIDE + z) * CORES + core


def routed(value, move, sections):
    pairs = []
    for section in sections:
        for x in range(SIDE):
            for y in range(SIDE):
                for z in range(SIDE):
                    for core in range(CORES):
                        here = (section, x, y, z, core)
                        pairs.append((place(*here), place(*move(*here))))
    return lax.ppermute(value, AXES, pairs)


def along_x(k):
    return lambda s, x, y, z, c: (s, (x + k) % SIDE, y, z, c)


def along_y(k):
    return lambda s, x, y, z, c: (s, x, (y + k) % SIDE, z, c)


def across_z(k):
    return lambda s, x, y, z, c: (s, x, y, z ^ k, c)


def other_core(s, x, y, z, c):
    return (s, x, y, z, 1 - c)


def hop(to_section):
    return lambda s, x, y, z, c: (s if to_section is None else to_section, (x - z) % SIDE, y, x, c)


def first_step(k):
    return lambda s, x, y, z, c: (along_y if s == 1 else along_x)(k)(s, x, y, z, c)


def dot(left, right, left_dim, right_dim):
    return lax.dot_general(
        left, right, (((left_dim,), (right_dim,)), ((), ())), preferred_element_type=f32
    )


def call(body, outs, args, at, grid=None, ins=None, out_specs=None, scratch=(), flops=0):
    whole = lambda a: pl.BlockSpec(a.shape, lambda *_, n=len(a.shape): (0,) * n)
    grid = grid or (1,)
    ins = [s or whole(a) for s, a in zip(ins or [None] * len(args), args)]
    out_specs = [s or whole(o) for s, o in zip(out_specs or [None] * len(outs), outs)]
    moved = sum(a.size * a.dtype.itemsize for a in (*args, *outs))
    return pl.pallas_call(
        body,
        grid_spec=pltpu.PrefetchScalarGridSpec(
            num_scalar_prefetch=1, grid=grid, in_specs=ins, out_specs=out_specs, scratch_shapes=list(scratch)
        ),
        out_shape=list(outs),
        compiler_params=pltpu.CompilerParams(vmem_limit_bytes=VMEM),
        cost_estimate=pl.CostEstimate(flops=flops, bytes_accessed=moved, transcendentals=0),
    )(at, *args)


def struct(shape, dtype=bf16):
    return jax.ShapeDtypeStruct(shape, dtype)


def behind(index, k):
    return lax.rem(index + SIDE - k, SIDE)


def span(index, size):
    return pl.ds(pl.multiple_of(index * size, size), size)


def rows_body(at, own, mine, theirs, w0, w1, w2, w3, out, piece, u):
    k = pl.program_id(0)
    y, z, core = at[1], at[2], at[3]
    half = mine.shape[1]
    fine = w0.shape[1]

    @pl.when(k == 0)
    def _():
        u[...] = own[...]

    @pl.when(k > 0)
    def _():
        u[span(core, half), :] = mine[0]
        u[span(1 - core, half), :] = theirs[0]

    @pl.when(k == z)
    def _():
        piece[...] = u[:, span(core, piece.shape[1])]

    total = None
    for j, w in enumerate((w0, w1, w2, w3)):
        term = dot(u[:, span(behind(y, j), fine)], w[...], 1, 1)
        total = term if total is None else total + term
    out[0] = total.astype(bf16)


def entering(grad, leading, c_rows, totals, states):
    size = totals.shape[0]
    scaled = (grad.astype(f32) * leading).astype(bf16)
    summed = dot(scaled, c_rows, 0, 0).astype(bf16)
    states[:, : states.shape[1] - totals.shape[1], :] = summed.reshape(
        size, summed.shape[0] // size, summed.shape[1]
    )
    states[:, states.shape[1] - totals.shape[1] :, :] = totals


def sum_body(at, own, r1, r2, r3, leading, c_rows, totals, grad, states):
    total = own[0].astype(f32)
    for r in (r1, r2, r3):
        total = total + r[...].astype(f32)
    rounded = total.astype(bf16)
    grad[...] = rounded
    entering(rounded, leading[...], c_rows[...], totals[...], states)


def lower_body(at, p0, p1, p2, p3, other, w0, w1, w2, w3, leading, c_rows, totals, grad, states, u):
    x, y, z, core = at[0], at[1], at[2], at[3]
    share = p0.shape[1]
    block = share * CORES
    fine = block // SIDE

    @pl.when(pl.program_id(0) == 0)
    def _():
        for q, part in enumerate((p0, p1, p2, p3)):
            base = (z ^ q) * CORES
            u[:, span(base + core, share)] = part[...]
            u[:, span(base + 1 - core, share)] = other[q]

    total = None
    for k, w in enumerate((w0, w1, w2, w3)):
        for j in range(SIDE):
            columns = u[:, span(behind(x, j) * SIDE + behind(y, k), fine)]
            term = dot(columns, w[j], 1, 1)
            total = term if total is None else total + term
    rounded = total.astype(bf16)
    grad[...] = rounded
    entering(rounded, leading[...], c_rows[...], totals[...], states)


def scan_body(at, states, exits):
    count, size, _ = exits.shape
    held = jnp.zeros(exits.shape[1:], f32)
    for k in range(count - 1, -1, -1):
        exits[k] = held.astype(bf16)
        total = states[k, size : size + 16, :].astype(f32)
        held = (total[0:1] + total[1:2]) * held + states[k, :size, :].astype(f32)


def within_body(at, grad, x_rows, kernel, mixed, leading, entry, b_rows, c_rows, skip, out, bc, weights):
    step = pl.program_id(0)
    pair = grad[...]
    x_pair = x_rows[...]
    low = lax.broadcasted_iota(jnp.int32, pair.shape, 1) < pair.shape[1] // 2
    none = jnp.zeros_like(pair)
    first = jnp.where(low, pair, none)
    second = jnp.where(low, none, pair)
    weighted = kernel[0].astype(f32) * dot(first, x_pair, 1, 1)
    weighted = weighted + kernel[1].astype(f32) * dot(second, x_pair, 1, 1)
    wide = pair.astype(f32)
    inside = jnp.where(low, dot(mixed[0], pair, 0, 0), dot(mixed[1], pair, 0, 0))
    out[...] = inside + skip[...] * wide
    from_entry = dot((wide * leading[...]).astype(bf16), entry[...], 1, 0)
    size = b_rows.shape[1]

    @pl.when(step == 0)
    def _():
        weights[...] = weighted
        bc[:, size:] = from_entry

    @pl.when(step > 0)
    def _():
        weights[...] += weighted
        bc[:, size:] += from_entry

    @pl.when(step == pl.num_programs(0) - 1)
    def _():
        rounded = weights[...].astype(bf16)
        bc[:, :size] = dot(rounded, c_rows[...], 0, 0)
        bc[:, size:] += dot(rounded, b_rows[...], 1, 0)


def finish_body(at, inside, bc, trailing, x_trailing, b_rows, leaving, out):
    inner = inside.shape[1]
    size = b_rows.shape[1]
    width = 256
    grad_b = bc[:, :size]
    for t in range(inner // width):
        columns = slice(t * width, (t + 1) * width)
        state = leaving[columns, :]
        gained = trailing[:, columns] * dot(b_rows[...], state, 1, 1)
        out[:, columns] = (inside[:, columns] + gained).astype(bf16)
        grad_b = grad_b + dot(x_trailing[:, columns], state, 1, 0)
    out[:, inner : inner + size] = grad_b.astype(bf16)
    out[:, inner + size :] = bc[:, size:].astype(bf16)


def back_body(at, g0, g1, g2, g3, weights, keep, give, u, g):
    k = pl.program_id(0)
    y, core = at[1], at[3]
    fine = weights.shape[1]
    share = keep.shape[2]
    for i, part in enumerate((g0, g1, g2, g3)):

        @pl.when(k == i)
        def _():
            g[...] = part[...]

    for j in range(SIDE):
        u[:, span(behind(y, j), fine)] = dot(g[...], weights[j], 1, 1).astype(bf16)
    keep[0] = u[:, span(core, share)]
    give[0] = u[:, span(1 - core, share)]


def whole_body(at, g, w0, w1, w2, w3, keep, give):
    x, y, z, core = at[0], at[1], at[2], at[3]
    fine = w0.shape[1]
    column = behind(y, pl.program_id(0))
    for k, w in enumerate((w0, w1, w2, w3)):
        q = z ^ behind(x, k)
        term = dot(g[...], w[0], 1, 1).astype(bf16)
        columns = span(lax.rem(column, CORES), fine)

        @pl.when(column // CORES == core)
        def _():
            keep[q, :, columns] = term

        @pl.when(column // CORES != core)
        def _():
            give[q, :, columns] = term


def pair_body(at, keep, got, s1, s2, s3):
    for q, out in ((1, s1), (2, s2), (3, s3)):
        out[...] = (keep[q].astype(f32) + got[q].astype(f32)).astype(bf16)


def total_body(at, keep, got, r1, r2, r3, upstream, out):
    total = keep[0].astype(f32) + got[0].astype(f32)
    for r in (r1, r2, r3):
        total = total + r[...].astype(f32)
    out[...] = (total + upstream[...].astype(f32)).astype(bf16)


def decay_tables(decay_rates):
    cumulative = jnp.cumsum(decay_rates, axis=1)
    spread = cumulative[:, :, None] - cumulative[:, None, :]
    length = decay_rates.shape[1]
    lower = jnp.arange(length)[:, None] >= jnp.arange(length)[None, :]
    kernel = jnp.where(lower[None], jnp.exp(jnp.minimum(spread, 0.0)), 0.0)
    return cumulative, kernel


def local(grad_out, w_out, w_in, w_bc, x_act, bc_act, decay, skip_gain, state_in):
    section = lax.axis_index("section")
    ctx = lax.axis_index("ctx")
    heads_at = lax.axis_index("heads")
    x, y = ctx // SIDE, ctx % SIDE
    z, core = heads_at // CORES, heads_at % CORES
    at = jnp.stack([x, y, z, core]).astype(jnp.int32)
    rows, width = grad_out.shape
    block = width // SIDE
    share = block // CORES
    fine = w_out.shape[2]
    half = rows // CORES
    head_count, head_size, state_size = state_in.shape[2:]
    inner = head_count * head_size
    outer = inner + 2 * state_size
    tiles = inner // 256
    tile_heads = head_count // tiles
    pad = 16

    out_parts = [w_out[0]] + [routed(w_out[0], first_step(k), BOTH) for k in (1, 2, 3)]

    pieces = []
    for k in (1, 2, 3):
        piece = lax.dynamic_slice(grad_out, (half * core, block * ((x + k) % SIDE)), (half, block))
        pieces.append(routed(piece, along_x(k), (1,)))
    mine = jnp.stack(pieces)
    theirs = routed(mine, other_core, (1,))

    back = jnp.concatenate([w_in[0], w_bc[0]], axis=1)
    back, out_parts = lax.optimization_barrier((back, out_parts))
    back_set = jnp.stack([back] + [routed(back, along_y(k), BOTH) for k in (1, 2, 3)])
    out_set = jnp.stack(out_parts)

    cumulative, kernel = decay_tables(decay[0])
    leading = jnp.repeat(jnp.exp(cumulative).T, head_size, axis=1)
    trailing = jnp.repeat(jnp.exp(cumulative[:, -1:] - cumulative).T, head_size, axis=1)
    b_rows = bc_act[0][:, :state_size]
    c_rows = bc_act[0][:, state_size:]
    common = dot(c_rows, b_rows, 1, 1)
    mixed = (kernel * common[None]).astype(bf16)
    kernel = kernel.astype(bf16)
    x_rows = x_act[0]
    x_trailing = (x_rows.astype(f32) * trailing).astype(bf16)
    entry = state_in[0, 0].reshape(inner, state_size).astype(bf16)
    skip = jnp.repeat(skip_gain[0], head_size)[None]
    total = jnp.exp(cumulative[:, -1])
    high = total.astype(bf16)
    low = (total - high.astype(f32)).astype(bf16)
    totals = jnp.concatenate(
        [high[:, None], low[:, None], jnp.zeros((head_count, pad - 2), bf16)], axis=1
    )
    totals = jnp.broadcast_to(totals[:, :, None], (head_count, pad, state_size))

    per_tile = pl.BlockSpec((rows, 256), lambda t, p: (0, t))
    tile_totals = pl.BlockSpec((tile_heads, pad, state_size), lambda t, p: (t, 0, 0))
    tile_states = pl.BlockSpec((tile_heads, head_size + pad, state_size), lambda t, p: (t, 0, 0))
    state_shape = struct((head_count, head_size + pad, state_size))

    def mixer(grad_ssd, states):
        arrived = lax.all_to_all(states, "ctx", 0, 0)
        (exits,) = call(scan_body, [struct((head_count, head_size, state_size))], [arrived], at)
        leaving = lax.all_to_all(exits, "ctx", 0, 0).reshape(inner, state_size)
        pair = pl.BlockSpec((rows, 128), lambda t, p: (0, t))
        table = pl.BlockSpec((2, rows, rows), lambda t, p: (t, 0, 0))
        inside, bc = call(
            within_body,
            [struct((rows, inner), f32), struct((rows, 2 * state_size), f32)],
            [grad_ssd, x_rows, kernel, mixed, leading, entry, b_rows, c_rows, skip],
            at,
            grid=(inner // 128,),
            ins=[
                pair, pair, table, table, pair,
                pl.BlockSpec((128, state_size), lambda t, p: (t, 0)),
                None, None,
                pl.BlockSpec((1, 128), lambda t, p: (0, t)),
            ],
            out_specs=[pair, None],
            scratch=[pltpu.VMEM((rows, rows), f32)],
            flops=4 * rows * rows * inner,
        )
        (grads,) = call(
            finish_body,
            [struct((rows, outer))],
            [inside, bc, trailing, x_trailing, b_rows, leaving],
            at,
            flops=4 * rows * inner * state_size,
        )
        return grads

    def over_heads(keep, give, upstream, sections):
        got = routed(give, other_core, sections)
        chunk = struct((rows, share))
        sent = call(pair_body, [chunk] * 3, [keep, got], at)
        received = [routed(s, across_z(k), sections) for k, s in zip((1, 2, 3), sent)]
        one = pl.BlockSpec((1, rows, share), lambda t, p: (0, 0, 0))
        (total,) = call(
            total_body, [chunk], [keep, got, *received, upstream], at, ins=[one, one] + [None] * 4
        )
        return total

    third = pl.BlockSpec((1, half, block), lambda k, p: (jnp.maximum(k - 1, 0), 0, 0))
    partial, own = call(
        rows_body,
        [struct((SIDE, rows, inner)), struct((rows, share))],
        [grad_out, mine, theirs, *out_parts],
        at,
        grid=(SIDE,),
        ins=[pl.BlockSpec((rows, block), lambda k, p: (0, p[0])), third, third] + [None] * 4,
        out_specs=[pl.BlockSpec((1, rows, inner), lambda k, p: (k, 0, 0)), None],
        scratch=[pltpu.VMEM((rows, block), bf16)],
        flops=2 * SIDE * rows * block * inner,
    )
    received = [routed(partial[k], along_x(-k), (1,)) for k in (1, 2, 3)]
    grad_ssd, states = call(
        sum_body,
        [struct((rows, inner)), state_shape],
        [partial, *received, leading, c_rows, totals],
        at,
        grid=(tiles,),
        ins=[pl.BlockSpec((1, rows, 256), lambda t, p: (0, 0, t))] + [per_tile] * 4 + [None, tile_totals],
        out_specs=[per_tile, tile_states],
        flops=2 * rows * inner * state_size,
    )
    grads = mixer(grad_ssd, states)

    out_whole = [routed(out_set, along_y(k), (0,)) for k in (1, 2, 3)]
    back_whole = [routed(back_set, along_x(k), (0,)) for k in (1, 2, 3)]

    grads_all = [grads] + [routed(grads, along_x(k), (1,)) for k in (1, 2, 3)]
    grads_all, out_whole, back_whole = lax.optimization_barrier((grads_all, out_whole, back_whole))
    chunks = struct((SIDE, rows, share))
    by_z = pl.BlockSpec((1, rows, share), lambda k, p: (p[2] ^ k, 0, 0))
    keep, give = call(
        back_body,
        [chunks, chunks],
        [*grads_all, back_set],
        at,
        grid=(SIDE,),
        out_specs=[by_z, by_z],
        scratch=[pltpu.VMEM((rows, block), bf16), pltpu.VMEM((rows, outer), bf16)],
        flops=2 * SIDE * rows * block * outer,
    )
    middle = over_heads(keep, give, own, (1,))

    arrived = routed(middle, hop(0), (1,))
    settled = routed(middle, hop(None), (1,))

    parts = [arrived] + [routed(arrived, across_z(k), (0,)) for k in (1, 2, 3)]
    other = routed(jnp.stack(parts), other_core, (0,))
    weights = pl.BlockSpec((SIDE, 256, fine), lambda t, p: (0, t, 0))
    grad_ssd, states = call(
        lower_body,
        [struct((rows, inner)), state_shape],
        [*parts, other, out_set, *out_whole, leading, c_rows, totals],
        at,
        grid=(tiles,),
        ins=[None] * 5 + [weights] * 4 + [per_tile, None, tile_totals],
        out_specs=[per_tile, tile_states],
        scratch=[pltpu.VMEM((rows, width), bf16)],
        flops=2 * rows * width * inner,
    )
    grads = mixer(grad_ssd, states)
    weights = pl.BlockSpec((1, fine, outer), lambda t, p: (t, 0, 0))
    keep, give = call(
        whole_body,
        [chunks, chunks],
        [grads, back_set, *back_whole],
        at,
        grid=(SIDE,),
        ins=[None] + [weights] * 4,
        flops=2 * rows * width * outer,
    )
    result = over_heads(keep, give, arrived, (0,))
    return jnp.where(section == 1, settled, result)[None]


def solution(mesh):
    placed = (
        P("ctx", None),
        P("section", "heads", "ctx"),
        P("section", "ctx", "heads"),
        P("section", "ctx", "heads"),
        P("section", "ctx", "heads"),
        P("section", "ctx", "heads"),
        P("section", "heads", "ctx"),
        P("section", "heads"),
        P("section", "ctx", "heads", None, None),
    )
    return jax.shard_map(
        local, mesh=mesh, in_specs=placed, out_specs=P("section", "ctx", "heads"), check_vma=False
    )
```

```python
import jax
import jax.numpy as jnp
from jax import lax
from jax.experimental import pallas as pl
from jax.experimental.pallas import tpu as pltpu
from jax.sharding import PartitionSpec as P

SIDE = 4
CORES = 2
BOTH = (0, 1)
AXES = ("section", "ctx", "heads")
VMEM = 20 * 1024 * 1024
bf16, f32 = jnp.bfloat16, jnp.float32


def place(section, x, y, z, core):
    return (((section * SIDE + x) * SIDE + y) * SIDE + z) * CORES + core


def routed(value, move, sections):
    pairs = []
    for section in sections:
        for x in range(SIDE):
            for y in range(SIDE):
                for z in range(SIDE):
                    for core in range(CORES):
                        here = (section, x, y, z, core)
                        pairs.append((place(*here), place(*move(*here))))
    return lax.ppermute(value, AXES, pairs)


def first_half(value, axis):
    return lax.slice_in_dim(value, 0, value.shape[axis] // 2, axis=axis)


def second_half(value, axis):
    return lax.slice_in_dim(value, value.shape[axis] // 2, value.shape[axis], axis=axis)


def sides(value, along, sections):
    return [routed(value, along(k), sections) for k in (1, 3)]


def far(both, along, sections, axis):
    before, after = both
    return [
        routed(first_half(before, axis), along(1), sections),
        routed(second_half(after, axis), along(3), sections),
    ]


def along_x(k):
    return lambda s, x, y, z, c: (s, (x + k) % SIDE, y, z, c)


def along_y(k):
    return lambda s, x, y, z, c: (s, x, (y + k) % SIDE, z, c)


def across_z(k):
    return lambda s, x, y, z, c: (s, x, y, z ^ k, c)


def other_core(s, x, y, z, c):
    return (s, x, y, z, 1 - c)


def hop(to_section):
    return lambda s, x, y, z, c: (s if to_section is None else to_section, (x - z) % SIDE, y, x, c)


def first_step(k):
    return lambda s, x, y, z, c: (along_y if s == 1 else along_x)(k)(s, x, y, z, c)


def dot(left, right, left_dim, right_dim):
    return lax.dot_general(
        left, right, (((left_dim,), (right_dim,)), ((), ())), preferred_element_type=f32
    )


def call(body, outs, args, at, scratch=(), flops=0, remote=()):
    moved = sum(a.size * a.dtype.itemsize for a in (*args, *outs))
    vmem = pl.BlockSpec(memory_space=pltpu.VMEM)
    ins = [pl.BlockSpec(memory_space=pl.ANY) if i in remote else vmem for i in range(len(args))]
    return pl.pallas_call(
        body,
        in_specs=[pl.BlockSpec(memory_space=pltpu.SMEM)] + ins,
        out_specs=[vmem] * len(outs),
        out_shape=list(outs),
        scratch_shapes=list(scratch),
        compiler_params=pltpu.CompilerParams(vmem_limit_bytes=VMEM),
        cost_estimate=pl.CostEstimate(flops=flops, bytes_accessed=moved, transcendentals=0),
    )(at, *args)


def struct(shape, dtype=bf16):
    return jax.ShapeDtypeStruct(shape, dtype)


def behind(index, k):
    return lax.rem(index + SIDE - k, SIDE)


def span(index, size):
    return pl.ds(pl.multiple_of(index * size, size), size)


def tables_body(
    at, decay, bc_rows, x_rows, state,
    kernel, mixed, x_heads, x_trailing, entry, leading, trailing, totals, b_cols, c_cols, c_rows,
):
    count, length = decay.shape
    size = b_cols.shape[0]
    each = x_heads.shape[0] // count
    exact = lax.Precision.HIGHEST
    earlier = lax.broadcasted_iota(jnp.int32, (length, length), 0)
    later = lax.broadcasted_iota(jnp.int32, (length, length), 1)
    lower = earlier >= later
    inner = (((1,), (0,)), ((), ()))
    last = (((1,), (1,)), ((), ()))
    rates = decay[...]
    sums = lax.dot_general(
        rates, (earlier <= later).astype(f32), inner, precision=exact, preferred_element_type=f32
    )
    columns = lax.dot_general(
        lower.astype(f32), rates, last, precision=exact, preferred_element_type=f32
    )
    b_part, c_part = bc_rows[:, :size], bc_rows[:, size:]
    common = dot(c_part, b_part, 1, 1)
    b_cols[...] = b_part.astype(f32).T.astype(bf16)
    c_cols[...] = c_part.astype(f32).T.astype(bf16)
    c_rows[...] = c_part
    lead = jnp.exp(sums)
    trail = jnp.exp(sums[:, length - 1 :] - sums)
    leading[...] = lead
    trailing[...] = trail
    first = lax.broadcasted_iota(jnp.int32, totals.shape[1:], 0) == 0
    for head in range(count):
        spread = columns[:, head : head + 1] - sums[head : head + 1, :]
        weights = jnp.where(lower, jnp.exp(jnp.minimum(spread, 0.0)), 0.0)
        kernel[head] = weights.astype(bf16)
        mixed[head] = (weights * common).astype(bf16)
        total = jnp.broadcast_to(lead[head : head + 1, length - 1 :], totals.shape[1:])
        high = total.astype(bf16).astype(f32)
        totals[head] = jnp.where(first, high, total - high).astype(bf16)
    for pair in range(count // 2):
        both = slice(pair * 2 * each, (pair + 1) * 2 * each)
        x_pair = x_rows[:, both].astype(f32).T
        x_heads[both, :] = x_pair.astype(bf16)
        for i in range(2):
            head = 2 * pair + i
            own = slice(head * each, (head + 1) * each)
            x_trailing[own, :] = (
                x_pair[i * each : (i + 1) * each, :] * trail[head : head + 1, :]
            ).astype(bf16)
        flat = jnp.concatenate([state[2 * pair], state[2 * pair + 1]], axis=0)
        entry[:, both] = flat.T.astype(bf16)


def rows_body(at, own, mine, theirs, w0, w1, wl, wh, w3, o0, o1, o2, o3, piece, u):
    y, z, core = at[1], at[2], at[3]
    fine = w0.shape[1]
    rows = mine.shape[1]
    half = wl.shape[0]
    u[0] = own[...]
    for k in (1, 2, 3):
        u[k, span(core, rows), :] = mine[k - 1]
        u[k, span(1 - core, rows), :] = theirs[k - 1]
    piece[...] = u[z, :, span(core, piece.shape[0])].astype(f32).T.astype(bf16)
    for k, out in enumerate((o0, o1, o2, o3)):
        total = None
        for j, w in enumerate((w0, w1, None, w3)):
            columns = u[k, :, span(behind(y, j), fine)]
            if w is None:
                term = jnp.concatenate([dot(wl[...], columns, 1, 1), dot(wh[...], columns, 1, 1)], axis=0)
            else:
                term = dot(w[...], columns, 1, 1)
            total = term if total is None else total + term
        out[...] = total.astype(bf16)


def entering(grad, leading, c_rows, totals, states):
    count = totals.shape[0]
    each = grad.shape[0] // count
    wide = grad.astype(f32)
    scaled = [
        (wide[h * each : (h + 1) * each] * leading[h : h + 1, :]).astype(bf16) for h in range(count)
    ]
    summed = dot(jnp.concatenate(scaled, axis=0), c_rows[...], 1, 0).astype(bf16)
    for h in range(count):
        states[h, :each, :] = summed[h * each : (h + 1) * each]
        states[h, each:, :] = totals[h]


def sum_body(at, own, r1, r2, r3, leading, c_rows, totals, grad, states):
    total = own[...].astype(f32)
    for r in (r1, r2, r3):
        total = total + r[...].astype(f32)
    rounded = total.astype(bf16)
    grad[...] = rounded
    entering(rounded, leading, c_rows, totals, states)


def lower_body(
    at, p0, p1, p2, p3, other, w0, w1, wl, wh, w3, leading, c_rows, totals, grad, states, u
):
    x, y, z, core = at[0], at[1], at[2], at[3]
    share = p0.shape[0]
    fine = share * CORES // SIDE
    for q, part in enumerate((p0, p1, p2, p3)):
        base = (z ^ q) * CORES
        u[span(base + core, share), :] = part[...]
        u[span(base + 1 - core, share), :] = other[q]
    total = None
    for k in range(SIDE):
        for j in range(SIDE):
            w = (w0, w1, wl if j < CORES else wh, w3)[k][j % CORES if k == 2 else j]
            rows = u[span(behind(x, j) * SIDE + behind(y, k), fine), :]
            term = dot(w, rows, 1, 0)
            total = term if total is None else total + term
    rounded = total.astype(bf16)
    grad[...] = rounded
    entering(rounded, leading, c_rows, totals, states)


def scan_body(at, states, exits):
    count, size, _ = exits.shape
    held = jnp.zeros(exits.shape[1:], f32)
    for k in range(count - 1, -1, -1):
        exits[k] = held.astype(bf16)
        total = states[k, size : size + 16, :].astype(f32)
        held = (total[0:1] + total[1:2]) * held + states[k, :size, :].astype(f32)


def block_body(
    at, grad, kernel, mixed, x_heads, x_trailing, leading, trailing, gain, entry, b_cols, c_cols, leaving,
    out, own_kernel, own_mixed, own_x, own_trailing, sems,
):
    copies = [
        pltpu.make_async_copy(source, target, sems.at[i])
        for i, (source, target) in enumerate(
            ((x_heads, own_x), (kernel, own_kernel), (mixed, own_mixed), (x_trailing, own_trailing))
        )
    ]
    for copy in copies:
        copy.start()
    count = leading.shape[0]
    inner = grad.shape[0]
    each = inner // count
    size = b_cols.shape[0]
    scaled = []
    for h in range(count):
        own = slice(h * each, (h + 1) * each)
        scaled.append((grad[own, :].astype(f32) * leading[h : h + 1, :]).astype(bf16))
    grad_c = dot(entry[...], jnp.concatenate(scaled, axis=0), 1, 0)
    gained = dot(leaving[...], b_cols[...], 1, 0)
    for copy in copies:
        copy.wait()
    weighted = None
    for h in range(count):
        own = slice(h * each, (h + 1) * each)
        g = grad[own, :]
        term = own_kernel[h].astype(f32) * dot(g, own_x[own, :], 0, 0)
        weighted = term if weighted is None else weighted + term
        inside = dot(g, own_mixed[h], 1, 0) + gain[h : h + 1, :] * g.astype(f32)
        out[own, :] = (inside + trailing[h : h + 1, :] * gained[own, :]).astype(bf16)
    rounded = weighted.astype(bf16)
    grad_b = dot(c_cols[...], rounded, 1, 0) + dot(leaving[...], own_trailing[...], 0, 0)
    out[inner : inner + size, :] = grad_b.astype(bf16)
    out[inner + size :, :] = (grad_c + dot(b_cols[...], rounded, 1, 1)).astype(bf16)


def to_halves(u, q, core, keep, give):
    share = keep.shape[1]
    keep[q] = u[span(core, share), :]
    give[q] = u[span(1 - core, share), :]


def back_body(at, g0, g1, gl, gh, g3, w0, w1, wl, wh, w3, keep, give, u, g2):
    y, z, core = at[1], at[2], at[3]
    fine, half = w0.shape[0], wl.shape[0]
    g2[: gl.shape[0], :] = gl[...]
    g2[gl.shape[0] :, :] = gh[...]
    for k, g in enumerate((g0, g1, g2, g3)):
        for j, w in enumerate((w0, w1, None, w3)):
            rows = span(behind(y, j), fine)
            if w is None:
                term = jnp.concatenate([dot(wl[...], g[...], 1, 0), dot(wh[...], g[...], 1, 0)], axis=0)
            else:
                term = dot(w[...], g[...], 1, 0)
            u[k, rows, :] = term.astype(bf16)
        to_halves(u.at[k], z ^ k, core, keep, give)


def whole_body(at, g, w0, w1, wl, wh, w3, keep, give, u):
    x, y, z, core = at[0], at[1], at[2], at[3]
    fine = w0.shape[1]
    for k in range(SIDE):
        for j in range(SIDE):
            w = (w0, w1, wl if j < CORES else wh, w3)[k][j % CORES if k == 2 else j]
            u[k, span(behind(y, j), fine), :] = dot(w, g[...], 1, 0).astype(bf16)
        to_halves(u.at[k], z ^ behind(x, k), core, keep, give)


def pair_body(at, keep, got, s1, s2, s3):
    for q, out in ((1, s1), (2, s2), (3, s3)):
        out[...] = (keep[q].astype(f32) + got[q].astype(f32)).astype(bf16)


def total_of(keep, got, received, upstream):
    total = keep[0].astype(f32) + got[0].astype(f32)
    for r in received:
        total = total + r[...].astype(f32)
    return total + upstream[...].astype(f32)


def total_body(at, keep, got, r1, r2, r3, upstream, out):
    out[...] = total_of(keep, got, (r1, r2, r3), upstream).astype(bf16)


def result_body(at, keep, got, r1, r2, r3, upstream, settled, out):
    total = total_of(keep, got, (r1, r2, r3), upstream).astype(bf16).astype(f32)
    chosen = jnp.where(at[4] == 1, settled[...].astype(f32), total)
    out[0] = chosen.T.astype(bf16)


def local(grad_out, w_out, w_in, w_bc, x_act, bc_act, decay, skip_gain, state_in):
    tie = lax.optimization_barrier
    section = lax.axis_index("section")
    ctx = lax.axis_index("ctx")
    heads_at = lax.axis_index("heads")
    x, y = ctx // SIDE, ctx % SIDE
    z, core = heads_at // CORES, heads_at % CORES
    at = jnp.stack([x, y, z, core, section]).astype(jnp.int32)
    rows, width = grad_out.shape
    block = width // SIDE
    share = block // CORES
    half = rows // CORES
    head_count, head_size, state_size = state_in.shape[2:]
    inner = head_count * head_size
    outer = inner + 2 * state_size
    pad = 16
    steps = (1, 2, 3)

    upstream = lax.dynamic_slice_in_dim(grad_out, block * x, block, 1)
    mine = []
    for k in steps:
        piece = lax.dynamic_slice(grad_out, (half * core, block * ((x + k) % SIDE)), (half, block))
        mine.append(routed(piece, along_x(k), (1,)))
    mine = jnp.stack(mine)
    theirs = routed(mine, other_core, (1,))

    out_sides = sides(w_out[0], first_step, BOTH)
    out_far = far(out_sides, first_step, BOTH, 0)
    back = jnp.concatenate([w_in[0], w_bc[0]], axis=1)

    (
        kernel, mixed, x_heads, x_trailing, entry, leading, trailing, totals, b_cols, c_cols, c_rows
    ) = call(
        tables_body,
        [
            struct((head_count, rows, rows)), struct((head_count, rows, rows)),
            struct((inner, rows)), struct((inner, rows)), struct((state_size, inner)),
            struct((head_count, rows), f32), struct((head_count, rows), f32),
            struct((head_count, pad, state_size)), struct((state_size, rows)),
            struct((state_size, rows)), struct((rows, state_size)),
        ],
        [decay[0], bc_act[0], x_act[0], state_in[0, 0]],
        at,
        flops=2 * rows * rows * inner,
    )
    gain = jnp.broadcast_to(skip_gain[0][:, None], (head_count, rows))
    out_sides, out_far, back, leading, gain = tie((out_sides, out_far, back, leading, gain))

    state_shape = struct((head_count, head_size + pad, state_size))

    def exchange(states):
        return lax.all_to_all(states, "ctx", 0, 0)

    def scanned(arrived):
        (exits,) = call(scan_body, [struct((head_count, head_size, state_size))], [arrived], at)
        return exits

    def within(grad_ssd, leaving):
        (grads,) = call(
            block_body,
            [struct((outer, rows))],
            [
                grad_ssd, kernel, mixed, x_heads, x_trailing, leading, trailing, gain, entry, b_cols, c_cols,
                leaving.reshape(inner, state_size),
            ],
            at,
            scratch=[
                pltpu.VMEM(kernel.shape, bf16), pltpu.VMEM(mixed.shape, bf16),
                pltpu.VMEM(x_heads.shape, bf16), pltpu.VMEM(x_trailing.shape, bf16),
                pltpu.SemaphoreType.DMA((4,)),
            ],
            flops=4 * rows * rows * inner,
            remote=(1, 2, 3, 4),
        )
        return grads

    chunk = struct((share, rows))
    chunks = struct((SIDE, share, rows))

    def over_heads(keep, give, sections):
        got = routed(give, other_core, sections)
        sent = call(pair_body, [chunk] * 3, [keep, got], at)
        return [keep, got] + [routed(s, across_z(k), sections) for k, s in zip(steps, sent)]

    *partial, own = call(
        rows_body,
        [struct((inner, rows))] * SIDE + [chunk],
        [upstream, mine, theirs, w_out[0], out_sides[0], *out_far, out_sides[1]],
        at,
        scratch=[pltpu.VMEM((SIDE, rows, block), bf16)],
        flops=2 * SIDE * rows * block * inner,
    )
    partial, back, out_sides, out_far = tie((partial, back, out_sides, out_far))
    received = [routed(partial[k], along_x(-k), (1,)) for k in steps]
    back_sides = sides(back, along_y, BOTH)
    out_set = jnp.stack([w_out[0], out_sides[0], jnp.concatenate(out_far, 0), out_sides[1]])
    received, back_sides, out_set = tie((received, back_sides, out_set))
    grad_ssd, states = call(
        sum_body,
        [struct((inner, rows)), state_shape],
        [partial[0], *received, leading, c_rows, totals],
        at,
        flops=2 * rows * inner * state_size,
    )

    states, back_sides, out_set = tie((states, back_sides, out_set))
    arrived = exchange(states)
    back_far = far(back_sides, along_y, BOTH, 0)
    whole_sides = sides(out_set, along_y, (0,))
    arrived, back_far, whole_sides = tie((arrived, back_far, whole_sides))
    exits = scanned(arrived)
    back_set = jnp.stack([back, back_sides[0], jnp.concatenate(back_far, 0), back_sides[1]])
    exits, back_set, whole_sides = tie((exits, back_set, whole_sides))
    leaving = exchange(exits)
    whole_far = far(whole_sides, along_y, (0,), 0)
    width_sides = sides(back_set, along_x, (0,))
    leaving, whole_far, width_sides = tie((leaving, whole_far, width_sides))
    grads = within(grad_ssd, leaving)

    grads_sides = sides(grads, along_x, (1,))
    grads_far = far(grads_sides, along_x, (1,), 0)
    wide = [pltpu.VMEM((SIDE, block, rows), bf16)]
    keep, give = call(
        back_body,
        [chunks, chunks],
        [
            grads, grads_sides[0], *grads_far, grads_sides[1],
            back, back_sides[0], *back_far, back_sides[1],
        ],
        at,
        scratch=wide + [pltpu.VMEM((outer, rows), bf16)],
        flops=2 * SIDE * rows * block * outer,
    )
    sums = over_heads(keep, give, (1,))
    (middle,) = call(total_body, [chunk], [*sums, own], at)

    arrived = routed(middle, hop(0), (1,))
    settled = routed(middle, hop(None), (1,))

    arrived, width_sides = tie((arrived, width_sides))
    width_far = far(width_sides, along_x, (0,), 0)
    parts = [arrived] + [routed(arrived, across_z(k), (0,)) for k in steps]
    other = routed(jnp.stack(parts), other_core, (0,))
    grad_ssd, states = call(
        lower_body,
        [struct((inner, rows)), state_shape],
        [*parts, other, out_set, whole_sides[0], *whole_far, whole_sides[1], leading, c_rows, totals],
        at,
        scratch=[pltpu.VMEM((width, rows), bf16)],
        flops=2 * rows * width * inner,
    )
    held, width_far, settled = tie((exchange(states), width_far, settled))
    grads = within(grad_ssd, exchange(scanned(held)))
    keep, give = call(
        whole_body,
        [chunks, chunks],
        [grads, back_set, width_sides[0], *width_far, width_sides[1]],
        at,
        scratch=wide,
        flops=2 * rows * width * outer,
    )
    sums = over_heads(keep, give, (0,))
    (result,) = call(result_body, [struct((1, rows, share))], [*sums, arrived, settled], at)
    return result


def solution(mesh):
    placed = (
        P("ctx", None),
        P("section", "heads", "ctx"),
        P("section", "ctx", "heads"),
        P("section", "ctx", "heads"),
        P("section", "ctx", "heads"),
        P("section", "ctx", "heads"),
        P("section", "heads", "ctx"),
        P("section", "heads"),
        P("section", "ctx", "heads", None, None),
    )
    return jax.shard_map(
        local, mesh=mesh, in_specs=placed, out_specs=P("section", "ctx", "heads"), check_vma=False
    )
```

```python
import jax
import jax.numpy as jnp
from jax import lax
from jax.experimental import pallas as pl
from jax.experimental.pallas import tpu as pltpu
from jax.sharding import PartitionSpec as P

SIDE = 4
CORES = 2
BOTH = (0, 1)
AXES = ("section", "ctx", "heads")
VMEM = 20 * 1024 * 1024
MOST = 54 * 1024 * 1024
bf16, f32 = jnp.bfloat16, jnp.float32


def place(section, x, y, z, core):
    return (((section * SIDE + x) * SIDE + y) * SIDE + z) * CORES + core


def routed(value, move, sections):
    pairs = []
    for section in sections:
        for x in range(SIDE):
            for y in range(SIDE):
                for z in range(SIDE):
                    for core in range(CORES):
                        here = (section, x, y, z, core)
                        pairs.append((place(*here), place(*move(*here))))
    return lax.ppermute(value, AXES, pairs)


def first_half(value, axis):
    return lax.slice_in_dim(value, 0, value.shape[axis] // 2, axis=axis)


def second_half(value, axis):
    return lax.slice_in_dim(value, value.shape[axis] // 2, value.shape[axis], axis=axis)


def sides(value, along, sections):
    return [routed(value, along(k), sections) for k in (1, 3)]


def far(both, along, sections, axis):
    before, after = both
    return [
        routed(first_half(before, axis), along(1), sections),
        routed(second_half(after, axis), along(3), sections),
    ]


def along_x(k):
    return lambda s, x, y, z, c: (s, (x + k) % SIDE, y, z, c)


def along_y(k):
    return lambda s, x, y, z, c: (s, x, (y + k) % SIDE, z, c)


def across_z(k):
    return lambda s, x, y, z, c: (s, x, y, z ^ k, c)


def other_core(s, x, y, z, c):
    return (s, x, y, z, 1 - c)


def hop(to_section):
    return lambda s, x, y, z, c: (s if to_section is None else to_section, x ^ z, y, x, c)


def first_step(k):
    return lambda s, x, y, z, c: (along_y if s == 1 else along_x)(k)(s, x, y, z, c)


def dot(left, right, left_dim, right_dim):
    return lax.dot_general(
        left, right, (((left_dim,), (right_dim,)), ((), ())), preferred_element_type=f32
    )


class Late:
    def __init__(self, source, held, sem):
        self.held, self.copy, self.waited = held, pltpu.make_async_copy(source, held, sem), False
        self.shape = held.shape

    def __getitem__(self, index):
        if not self.waited:
            self.copy.wait()
            self.waited = True
        return self.held[index]


def call(body, outs, args, at=None, scratch=(), flops=0, remote=(), away=(), vmem_limit=VMEM):
    moved = sum(a.size * a.dtype.itemsize for a in (*args, *outs))
    vmem, hbm = pl.BlockSpec(memory_space=pltpu.VMEM), pl.BlockSpec(memory_space=pltpu.HBM)
    own = [pltpu.VMEM(args[i].shape, args[i].dtype) for i in remote]
    own += [pltpu.VMEM(outs[i].shape, outs[i].dtype) for i in away]

    def kernel(*refs):
        refs = list(refs)
        first = refs[:1] if at is not None else []
        refs = refs[len(first) :]
        ins, results = refs[: len(args)], refs[len(args) : len(args) + len(outs)]
        held = refs[len(args) + len(outs) :]
        sems = held.pop() if own else None
        held, extra = held[: len(own)], held[len(own) :]
        late = []
        for n, i in enumerate(remote):
            late.append(Late(ins[i], held[n], sems.at[n]))
            late[-1].copy.start()
            ins[i] = late[-1]
        targets = list(results)
        for n, i in enumerate(away):
            results[i] = held[len(remote) + n]
        body(*first, *ins, *results, *extra)
        for operand in late:
            operand[...] if not operand.waited else None
        copies = [
            pltpu.make_async_copy(results[i], targets[i], sems.at[len(remote) + n])
            for n, i in enumerate(away)
        ]
        for copy in copies:
            copy.start()
        for copy in copies:
            copy.wait()

    return pl.pallas_call(
        kernel,
        in_specs=[pl.BlockSpec(memory_space=pltpu.SMEM)] * (at is not None)
        + [hbm if i in remote else vmem for i in range(len(args))],
        out_specs=[hbm if i in away else vmem for i in range(len(outs))],
        out_shape=list(outs),
        scratch_shapes=own + list(scratch) + ([pltpu.SemaphoreType.DMA((len(own),))] if own else []),
        compiler_params=pltpu.CompilerParams(vmem_limit_bytes=vmem_limit),
        cost_estimate=pl.CostEstimate(flops=flops, bytes_accessed=moved, transcendentals=0),
    )(*([at] if at is not None else []), *args)


def struct(shape, dtype=bf16):
    return jax.ShapeDtypeStruct(shape, dtype)


def behind(index, k):
    return lax.rem(index + SIDE - k, SIDE)


def span(index, size):
    return pl.ds(pl.multiple_of(index * size, size), size)


def tables_body(
    decay, bc_rows, x_rows, state,
    kernel, mixed, x_heads, x_trailing, entry, leading, trailing, totals, b_cols, c_cols, c_rows,
):
    count, length = decay.shape
    size = b_cols.shape[0]
    each = x_heads.shape[0] // count
    exact = lax.Precision.HIGHEST
    earlier = lax.broadcasted_iota(jnp.int32, (length, length), 0)
    later = lax.broadcasted_iota(jnp.int32, (length, length), 1)
    lower = earlier >= later
    inner = (((1,), (0,)), ((), ()))
    last = (((1,), (1,)), ((), ()))
    rates = decay[...]
    sums = lax.dot_general(
        rates, (earlier <= later).astype(f32), inner, precision=exact, preferred_element_type=f32
    )
    columns = lax.dot_general(
        lower.astype(f32), rates, last, precision=exact, preferred_element_type=f32
    )
    b_part, c_part = bc_rows[:, :size], bc_rows[:, size:]
    common = dot(c_part, b_part, 1, 1)
    b_cols[...] = b_part.astype(f32).T.astype(bf16)
    c_cols[...] = c_part.astype(f32).T.astype(bf16)
    c_rows[...] = c_part
    lead = jnp.exp(sums)
    trail = jnp.exp(sums[:, length - 1 :] - sums)
    leading[...] = lead
    trailing[...] = trail
    first = lax.broadcasted_iota(jnp.int32, totals.shape[1:], 0) == 0
    for head in range(count):
        spread = columns[:, head : head + 1] - sums[head : head + 1, :]
        weights = jnp.where(lower, jnp.exp(jnp.minimum(spread, 0.0)), 0.0)
        kernel[head] = weights.astype(bf16)
        mixed[head] = (weights * common).astype(bf16)
        total = jnp.broadcast_to(lead[head : head + 1, length - 1 :], totals.shape[1:])
        high = total.astype(bf16).astype(f32)
        totals[head] = jnp.where(first, high, total - high).astype(bf16)
    for pair in range(count // 2):
        both = slice(pair * 2 * each, (pair + 1) * 2 * each)
        x_pair = x_rows[:, both].astype(f32).T
        x_heads[both, :] = x_pair.astype(bf16)
        for i in range(2):
            head = 2 * pair + i
            own = slice(head * each, (head + 1) * each)
            x_trailing[own, :] = (
                x_pair[i * each : (i + 1) * each, :] * trail[head : head + 1, :]
            ).astype(bf16)
        flat = jnp.concatenate([state[2 * pair], state[2 * pair + 1]], axis=0)
        entry[:, both] = flat.T.astype(bf16)


def rows_body(at, u1, u2, u3, v1, v2, v3, w1, wl, wh, w3, w0, whole, o0, o1, o2, o3, piece, u):
    x, y, z, core = at[0], at[1], at[2], at[3]
    fine = w1.shape[1]
    rows = u1.shape[0]
    for k, mine, theirs in ((1, u1, v1), (2, u2, v2), (3, u3, v3)):
        u[k, span(core, rows), :] = mine[...]
        u[k, span(1 - core, rows), :] = theirs[...]
    u[0] = whole[:, span(x, u.shape[2])]
    piece[...] = u[behind(x, x ^ z), :, span(core, piece.shape[0])].astype(f32).T.astype(bf16)
    for k, out in enumerate((o0, o1, o2, o3)):
        total = None
        for j, w in enumerate((w0, w1, None, w3)):
            columns = u[k, :, span(behind(y, j), fine)]
            if w is None:
                term = jnp.concatenate([dot(wl[...], columns, 1, 1), dot(wh[...], columns, 1, 1)], axis=0)
            else:
                term = dot(w[...], columns, 1, 1)
            total = term if total is None else total + term
        out[...] = total.astype(bf16)


def entering(grad, leading, c_rows, totals, states):
    count = totals.shape[0]
    each = grad.shape[0] // count
    wide = grad.astype(f32)
    scaled = [
        (wide[h * each : (h + 1) * each] * leading[h : h + 1, :]).astype(bf16) for h in range(count)
    ]
    summed = dot(jnp.concatenate(scaled, axis=0), c_rows[...], 1, 0).astype(bf16)
    for h in range(count):
        states[h, :each, :] = summed[h * each : (h + 1) * each]
        states[h, each:, :] = totals[h]


def sum_body(own, r1, r2, r3, leading, c_rows, totals, grad, states):
    total = own[...].astype(f32)
    for r in (r1, r2, r3):
        total = total + r[...].astype(f32)
    rounded = total.astype(bf16)
    grad[...] = rounded
    entering(rounded, leading, c_rows, totals, states)


def lower_body(
    at, p0, p1, p2, p3, other, w0, w1, wl, wh, w3, leading, c_rows, totals, grad, states, u
):
    x, y, z, core = at[0], at[1], at[2], at[3]
    share = p0.shape[0]
    fine = share * CORES // SIDE
    for q, part in enumerate((p0, p1, p2, p3)):
        base = (z ^ q) * CORES
        u[span(base + core, share), :] = part[...]
        u[span(base + 1 - core, share), :] = other[q]
    total = None
    for k in range(SIDE):
        for j in range(SIDE):
            w = (w0, w1, wl if j < CORES else wh, w3)[k][j % CORES if k == 2 else j]
            rows = u[span(behind(x, j) * SIDE + behind(y, k), fine), :]
            term = dot(w, rows, 1, 0)
            total = term if total is None else total + term
    rounded = total.astype(bf16)
    grad[...] = rounded
    entering(rounded, leading, c_rows, totals, states)


def scan_body(states, exits):
    count, size, _ = exits.shape
    held = jnp.zeros(exits.shape[1:], f32)
    for k in range(count - 1, -1, -1):
        exits[k] = held.astype(bf16)
        total = states[k, size : size + 16, :].astype(f32)
        held = (total[0:1] + total[1:2]) * held + states[k, :size, :].astype(f32)


def block_body(
    grad, leading, entry, leaving, b_cols, x_heads, kernel, mixed, gain, trailing, x_trailing, c_cols, out
):
    count = leading.shape[0]
    inner = grad.shape[0]
    each = inner // count
    size = b_cols.shape[0]
    scaled = []
    for h in range(count):
        own = slice(h * each, (h + 1) * each)
        scaled.append((grad[own, :].astype(f32) * leading[h : h + 1, :]).astype(bf16))
    grad_c = dot(entry[...], jnp.concatenate(scaled, axis=0), 1, 0)
    gained = dot(leaving[...], b_cols[...], 1, 0)
    weighted = None
    for h in range(count):
        own = slice(h * each, (h + 1) * each)
        g = grad[own, :]
        term = kernel[h].astype(f32) * dot(g, x_heads[own, :], 0, 0)
        weighted = term if weighted is None else weighted + term
        inside = dot(g, mixed[h], 1, 0) + gain[h : h + 1, :] * g.astype(f32)
        out[own, :] = (inside + trailing[h : h + 1, :] * gained[own, :]).astype(bf16)
    rounded = weighted.astype(bf16)
    grad_b = dot(c_cols[...], rounded, 1, 0) + dot(leaving[...], x_trailing[...], 0, 0)
    out[inner : inner + size, :] = grad_b.astype(bf16)
    out[inner + size :, :] = (grad_c + dot(b_cols[...], rounded, 1, 1)).astype(bf16)


def to_halves(u, q, core, keep, give):
    share = keep.shape[1]
    keep[q] = u[span(core, share), :]
    give[q] = u[span(1 - core, share), :]


def back_body(at, g0, g1, gl, gh, g3, w0, w1, wl, wh, w3, keep, give, u, g2):
    x, y, z, core = at[0], at[1], at[2], at[3]
    fine = w0.shape[0]
    g2[: gl.shape[0], :] = gl[...]
    g2[gl.shape[0] :, :] = gh[...]
    for k, g in enumerate((g0, g1, g2, g3)):
        for j, w in enumerate((w0, w1, None, w3)):
            rows = span(behind(y, j), fine)
            if w is None:
                term = jnp.concatenate([dot(wl[...], g[...], 1, 0), dot(wh[...], g[...], 1, 0)], axis=0)
            else:
                term = dot(w[...], g[...], 1, 0)
            u[k, rows, :] = term.astype(bf16)
        to_halves(u.at[k], z ^ x ^ behind(x, k), core, keep, give)


def whole_body(at, g, w0, w1, wl, wh, w3, keep, give, u):
    x, y, z, core = at[0], at[1], at[2], at[3]
    fine = w0.shape[1]
    for k in range(SIDE):
        for j in range(SIDE):
            w = (w0, w1, wl if j < CORES else wh, w3)[k][j % CORES if k == 2 else j]
            u[k, span(behind(y, j), fine), :] = dot(w, g[...], 1, 0).astype(bf16)
        to_halves(u.at[k], z ^ behind(x, k), core, keep, give)


def pair_body(keep, got, s1, s2, s3):
    for q, out in ((1, s1), (2, s2), (3, s3)):
        out[...] = (keep[q].astype(f32) + got[q].astype(f32)).astype(bf16)


def total_of(keep, got, received, upstream):
    total = keep[0].astype(f32) + got[0].astype(f32)
    for r in received:
        total = total + r[...].astype(f32)
    return total + upstream[...].astype(f32)


def total_body(keep, got, r1, r2, r3, upstream, out):
    out[...] = total_of(keep, got, (r1, r2, r3), upstream).astype(bf16)


def result_body(at, keep, got, r1, r2, r3, upstream, settled, out):
    total = total_of(keep, got, (r1, r2, r3), upstream).astype(bf16).astype(f32)
    chosen = jnp.where(at[4] == 1, settled[...].astype(f32), total)
    out[0] = chosen.T.astype(bf16)


def local(grad_out, w_out, w_in, w_bc, x_act, bc_act, decay, skip_gain, state_in):
    tie = lax.optimization_barrier
    section = lax.axis_index("section")
    ctx = lax.axis_index("ctx")
    heads_at = lax.axis_index("heads")
    x, y = ctx // SIDE, ctx % SIDE
    z, core = heads_at // CORES, heads_at % CORES
    at = jnp.stack([x, y, z, core, section]).astype(jnp.int32)
    rows, width = grad_out.shape
    block = width // SIDE
    share = block // CORES
    half = rows // CORES
    head_count, head_size, state_size = state_in.shape[2:]
    inner = head_count * head_size
    outer = inner + 2 * state_size
    pad = 16
    steps = (1, 2, 3)

    out_sides = sides(w_out[0], first_step, BOTH)
    out_far = far(out_sides, first_step, BOTH, 0)
    mine = []
    for k in steps:
        piece = lax.dynamic_slice(grad_out, (half * core, block * ((x + k) % SIDE)), (half, block))
        mine.append(routed(piece, along_x(k), (1,)))
    theirs = [routed(piece, other_core, (1,)) for piece in mine]

    back = jnp.concatenate([w_in[0], w_bc[0]], axis=1)
    out_far, back = tie((out_far, back))
    back_sides = sides(back, along_y, BOTH)

    (
        kernel, mixed, x_heads, x_trailing, entry, leading, trailing, totals, b_cols, c_cols, c_rows
    ) = call(
        tables_body,
        [
            struct((head_count, rows, rows)), struct((head_count, rows, rows)),
            struct((inner, rows)), struct((inner, rows)), struct((state_size, inner)),
            struct((head_count, rows), f32), struct((head_count, rows), f32),
            struct((head_count, pad, state_size)), struct((state_size, rows)),
            struct((state_size, rows)), struct((rows, state_size)),
        ],
        [decay[0], bc_act[0], x_act[0], state_in[0, 0]],
        remote=range(4),
        flops=2 * rows * rows * inner,
    )
    gain = jnp.broadcast_to(skip_gain[0][:, None], (head_count, rows))
    out_sides, out_far, leading, gain = tie((out_sides, out_far, leading, gain))

    state_shape = struct((head_count, head_size + pad, state_size))

    def exchange(states):
        return lax.all_to_all(states, "ctx", 0, 0)

    def scanned(arrived):
        (exits,) = call(
            scan_body, [struct((head_count, head_size, state_size))], [arrived], away=(0,)
        )
        return exits

    def within(grad_ssd, leaving, vmem_limit=VMEM):
        (grads,) = call(
            block_body,
            [struct((outer, rows))],
            [
                grad_ssd, leading, entry, leaving.reshape(inner, state_size), b_cols, x_heads, kernel, mixed,
                gain, trailing, x_trailing, c_cols,
            ],
            flops=4 * rows * rows * inner,
            remote=range(12),
            vmem_limit=vmem_limit,
        )
        return grads

    chunk = struct((share, rows))
    chunks = struct((SIDE, share, rows))

    def over_heads(keep, give, sections):
        got = routed(give, other_core, sections)
        sent = call(pair_body, [chunk] * 3, [keep, got])
        return [keep, got] + [routed(s, across_z(k), sections) for k, s in zip(steps, sent)]

    *partial, own = call(
        rows_body,
        [struct((inner, rows))] * SIDE + [chunk],
        [*mine, *theirs, out_sides[0], *out_far, out_sides[1], w_out[0], grad_out],
        at,
        remote=(10, 11),
        scratch=[pltpu.VMEM((SIDE, rows, block), bf16)],
        flops=2 * SIDE * rows * block * inner,
    )
    partial, out_sides, out_far = tie((partial, out_sides, out_far))
    received = [routed(partial[k], along_x(-k), (1,)) for k in steps]
    back_far = far(back_sides, along_y, BOTH, 0)
    out_set = jnp.concatenate([w_out[0], out_sides[0], *out_far, out_sides[1]]).reshape(SIDE, inner, -1)
    received, back_far, out_set = tie((received, back_far, out_set))
    back_set = jnp.concatenate([back, back_sides[0], *back_far, back_sides[1]]).reshape(SIDE, -1, outer)
    grad_ssd, states = call(
        sum_body,
        [struct((inner, rows)), state_shape],
        [partial[0], *received, leading, c_rows, totals],
        remote=(4, 5, 6),
        away=(0, 1),
        flops=2 * rows * inner * state_size,
    )

    states, out_set, back_set = tie((states, out_set, back_set))
    arrived = exchange(states)
    whole_sides = sides(out_set, along_y, (0,))
    width_sides = sides(back_set, along_x, (0,))
    arrived, whole_sides, width_sides = tie((arrived, whole_sides, width_sides))
    exits = scanned(arrived)
    exits, whole_sides, width_sides = tie((exits, whole_sides, width_sides))
    leaving = exchange(exits)
    whole_far = far(whole_sides, along_y, (0,), 0)
    width_far = far(width_sides, along_x, (0,), 0)
    leaving, whole_far, width_far = tie((leaving, whole_far, width_far))
    grads = within(grad_ssd, leaving)

    grads_sides = sides(grads, along_x, (1,))
    grads_far = far(grads_sides, along_x, (1,), 0)
    wide = [pltpu.VMEM((SIDE, block, rows), bf16)]
    keep, give = call(
        back_body,
        [chunks, chunks],
        [
            grads, grads_sides[0], *grads_far, grads_sides[1],
            back, back_sides[0], *back_far, back_sides[1],
        ],
        at,
        scratch=wide + [pltpu.VMEM((outer, rows), bf16)],
        flops=2 * SIDE * rows * block * outer,
    )
    sums = over_heads(keep, give, (1,))
    (middle,) = call(total_body, [chunk], [*sums, own])

    arrived = routed(middle, hop(0), (1,))
    settled = routed(middle, hop(None), (1,))

    parts = [arrived] + [routed(arrived, across_z(k), (0,)) for k in steps]
    other = routed(jnp.stack(parts), other_core, (0,))
    grad_ssd, states = call(
        lower_body,
        [struct((inner, rows)), state_shape],
        [*parts, other, out_set, whole_sides[0], *whole_far, whole_sides[1], leading, c_rows, totals],
        at,
        scratch=[pltpu.VMEM((width, rows), bf16)],
        remote=range(10, 13),
        away=(0, 1),
        flops=2 * rows * width * inner,
    )
    held, settled = tie((exchange(states), settled))
    grads = within(grad_ssd, exchange(scanned(held)), MOST)
    keep, give = call(
        whole_body,
        [chunks, chunks],
        [grads, back_set, width_sides[0], *width_far, width_sides[1]],
        at,
        scratch=wide,
        flops=2 * rows * width * outer,
    )
    sums = over_heads(keep, give, (0,))
    (result,) = call(result_body, [struct((1, rows, share))], [*sums, arrived, settled], at)
    return result


def solution(mesh):
    placed = (
        P("ctx", None),
        P("section", "heads", "ctx"),
        P("section", "ctx", "heads"),
        P("section", "ctx", "heads"),
        P("section", "ctx", "heads"),
        P("section", "ctx", "heads"),
        P("section", "heads", "ctx"),
        P("section", "heads"),
        P("section", "ctx", "heads", None, None),
    )
    return jax.shard_map(
        local, mesh=mesh, in_specs=placed, out_specs=P("section", "ctx", "heads"), check_vma=False
    )
```

```python
import functools

import jax
import jax.numpy as jnp
from jax import lax
from jax.experimental import pallas as pl
from jax.experimental.pallas import tpu as pltpu
from jax.sharding import PartitionSpec as P

SIDE = 4
CORES = 2
BOTH = (0, 1)
AXES = ("section", "ctx", "heads")
VMEM = 20 * 1024 * 1024
MOST = 54 * 1024 * 1024
bf16, f32 = jnp.bfloat16, jnp.float32


def place(section, x, y, z, core):
    return (((section * SIDE + x) * SIDE + y) * SIDE + z) * CORES + core


def routed(value, move, sections):
    pairs = []
    for section in sections:
        for x in range(SIDE):
            for y in range(SIDE):
                for z in range(SIDE):
                    for core in range(CORES):
                        here = (section, x, y, z, core)
                        pairs.append((place(*here), place(*move(*here))))
    return lax.ppermute(value, AXES, pairs)


def first_half(value, axis):
    return lax.slice_in_dim(value, 0, value.shape[axis] // 2, axis=axis)


def second_half(value, axis):
    return lax.slice_in_dim(value, value.shape[axis] // 2, value.shape[axis], axis=axis)


def sides(value, along, sections):
    return [routed(value, along(k), sections) for k in (1, 3)]


def far(both, along, sections, axis):
    before, after = both
    return [
        routed(first_half(before, axis), along(1), sections),
        routed(second_half(after, axis), along(3), sections),
    ]


def along_x(k):
    return lambda s, x, y, z, c: (s, (x + k) % SIDE, y, z, c)


def along_y(k):
    return lambda s, x, y, z, c: (s, x, (y + k) % SIDE, z, c)


def across_z(k):
    return lambda s, x, y, z, c: (s, x, y, z ^ k, c)


def other_core(s, x, y, z, c):
    return (s, x, y, z, 1 - c)


def hop(to_section):
    return lambda s, x, y, z, c: (s if to_section is None else to_section, x ^ z, y, x, c)


def first_step(k):
    return lambda s, x, y, z, c: (along_y if s == 1 else along_x)(k)(s, x, y, z, c)


def dot(left, right, left_dim, right_dim):
    return lax.dot_general(
        left, right, (((left_dim,), (right_dim,)), ((), ())), preferred_element_type=f32
    )


class Late:
    def __init__(self, source, held, sem):
        self.held, self.copy, self.waited = held, pltpu.make_async_copy(source, held, sem), False
        self.shape = held.shape

    def __getitem__(self, index):
        if not self.waited:
            self.copy.wait()
            self.waited = True
        return self.held[index]


def call(body, outs, args, at=None, scratch=(), flops=0, remote=(), away=(), vmem_limit=VMEM):
    moved = sum(a.size * a.dtype.itemsize for a in (*args, *outs))
    vmem, hbm = pl.BlockSpec(memory_space=pltpu.VMEM), pl.BlockSpec(memory_space=pltpu.HBM)
    own = [pltpu.VMEM(args[i].shape, args[i].dtype) for i in remote]
    own += [pltpu.VMEM(outs[i].shape, outs[i].dtype) for i in away]

    def kernel(*refs):
        refs = list(refs)
        first = refs[:1] if at is not None else []
        refs = refs[len(first) :]
        ins, results = refs[: len(args)], refs[len(args) : len(args) + len(outs)]
        held = refs[len(args) + len(outs) :]
        sems = held.pop() if own else None
        held, extra = held[: len(own)], held[len(own) :]
        late = []
        for n, i in enumerate(remote):
            late.append(Late(ins[i], held[n], sems.at[n]))
            late[-1].copy.start()
            ins[i] = late[-1]
        targets = list(results)
        for n, i in enumerate(away):
            results[i] = held[len(remote) + n]
        body(*first, *ins, *results, *extra)
        for operand in late:
            if not operand.waited:
                operand[...]
        copies = [
            pltpu.make_async_copy(results[i], targets[i], sems.at[len(remote) + n])
            for n, i in enumerate(away)
        ]
        for copy in copies:
            copy.start()
        for copy in copies:
            copy.wait()

    return pl.pallas_call(
        kernel,
        in_specs=[pl.BlockSpec(memory_space=pltpu.SMEM)] * (at is not None)
        + [hbm if i in remote else vmem for i in range(len(args))],
        out_specs=[hbm if i in away else vmem for i in range(len(outs))],
        out_shape=list(outs),
        scratch_shapes=own + list(scratch) + ([pltpu.SemaphoreType.DMA((len(own),))] if own else []),
        compiler_params=pltpu.CompilerParams(vmem_limit_bytes=vmem_limit),
        cost_estimate=pl.CostEstimate(flops=flops, bytes_accessed=moved, transcendentals=0),
    )(*([at] if at is not None else []), *args)


def struct(shape, dtype=bf16):
    return jax.ShapeDtypeStruct(shape, dtype)


def behind(index, k):
    return lax.rem(index + SIDE - k, SIDE)


def span(index, size):
    return pl.ds(pl.multiple_of(index * size, size), size)


def tables_body(
    decay, bc_rows, x_rows, state,
    kernel, mixed, x_heads, x_trailing, entry, leading, trailing, totals, b_cols, c_cols, c_rows,
):
    count, length = decay.shape
    size = b_cols.shape[0]
    each = x_heads.shape[0] // count
    exact = lax.Precision.HIGHEST
    earlier = lax.broadcasted_iota(jnp.int32, (length, length), 0)
    later = lax.broadcasted_iota(jnp.int32, (length, length), 1)
    lower = earlier >= later
    inner = (((1,), (0,)), ((), ()))
    last = (((1,), (1,)), ((), ()))
    rates = decay[...]
    sums = lax.dot_general(
        rates, (earlier <= later).astype(f32), inner, precision=exact, preferred_element_type=f32
    )
    columns = lax.dot_general(
        lower.astype(f32), rates, last, precision=exact, preferred_element_type=f32
    )
    b_part, c_part = bc_rows[:, :size], bc_rows[:, size:]
    common = dot(c_part, b_part, 1, 1)
    b_cols[...] = b_part.astype(f32).T.astype(bf16)
    c_cols[...] = c_part.astype(f32).T.astype(bf16)
    c_rows[...] = c_part
    lead = jnp.exp(sums)
    trail = jnp.exp(sums[:, length - 1 :] - sums)
    leading[...] = lead
    trailing[...] = trail
    first = lax.broadcasted_iota(jnp.int32, totals.shape[1:], 0) == 0
    for head in range(count):
        spread = columns[:, head : head + 1] - sums[head : head + 1, :]
        weights = jnp.where(lower, jnp.exp(jnp.minimum(spread, 0.0)), 0.0)
        kernel[head] = weights.astype(bf16)
        mixed[head] = (weights * common).astype(bf16)
        total = jnp.broadcast_to(lead[head : head + 1, length - 1 :], totals.shape[1:])
        high = total.astype(bf16).astype(f32)
        totals[head] = jnp.where(first, high, total - high).astype(bf16)
    for pair in range(count // 2):
        both = slice(pair * 2 * each, (pair + 1) * 2 * each)
        x_pair = x_rows[:, both].astype(f32).T
        x_heads[both, :] = x_pair.astype(bf16)
        for i in range(2):
            head = 2 * pair + i
            own = slice(head * each, (head + 1) * each)
            x_trailing[own, :] = (
                x_pair[i * each : (i + 1) * each, :] * trail[head : head + 1, :]
            ).astype(bf16)
        flat = jnp.concatenate([state[2 * pair], state[2 * pair + 1]], axis=0)
        entry[:, both] = flat.T.astype(bf16)


def rows_body(at, own, u1, u2, v2, u3, w1, wl, wh, w3, w0, o0, o1, o2, o3, piece, u):
    x, y, z, core = at[0], at[1], at[2], at[3]
    fine = w1.shape[1]
    half = u2.shape[0]
    u[0] = own[...]
    u[1] = u1[...]
    u[2, span(core, half), :] = u2[...]
    u[2, span(1 - core, half), :] = v2[...]
    u[3] = u3[...]
    piece[...] = u[behind(x, x ^ z), :, span(core, piece.shape[0])].astype(f32).T.astype(bf16)
    for k, out in enumerate((o0, o1, o2, o3)):
        total = None
        for j, w in enumerate((w0, w1, None, w3)):
            columns = u[k, :, span(behind(y, j), fine)]
            if w is None:
                term = jnp.concatenate([dot(wl[...], columns, 1, 1), dot(wh[...], columns, 1, 1)], axis=0)
            else:
                term = dot(w[...], columns, 1, 1)
            total = term if total is None else total + term
        out[...] = total.astype(bf16)


def entering(grad, leading, c_rows, totals, states):
    count = totals.shape[0]
    each = grad.shape[0] // count
    wide = grad.astype(f32)
    scaled = [
        (wide[h * each : (h + 1) * each] * leading[h : h + 1, :]).astype(bf16) for h in range(count)
    ]
    summed = dot(jnp.concatenate(scaled, axis=0), c_rows[...], 1, 0).astype(bf16)
    for h in range(count):
        states[h, :each, :] = summed[h * each : (h + 1) * each]
        states[h, each:, :] = totals[h]


def sum_body(own, r1, r2, r3, leading, c_rows, totals, grad, states):
    total = own[...].astype(f32)
    for r in (r1, r2, r3):
        total = total + r[...].astype(f32)
    rounded = total.astype(bf16)
    grad[...] = rounded
    entering(rounded, leading, c_rows, totals, states)


def lower_body(
    at, a0, a1, a2, a3, b0, b1, b2, b3, other_a, other_b, w0, w1, wl, wh, w3, leading, c_rows, totals, grad, states, u
):
    x, y, z, core = at[0], at[1], at[2], at[3]
    fine = a0.shape[0]
    for q in range(SIDE):
        base = (z ^ q) * CORES
        for i, (parts, other) in enumerate((((a0, a1, a2, a3), other_a), ((b0, b1, b2, b3), other_b))):
            u[span((base + core) * 2 + i, fine), :] = parts[q][...]
            u[span((base + 1 - core) * 2 + i, fine), :] = other[q]
    total = None
    for k in range(SIDE):
        for j in range(SIDE):
            w = (w0, w1, wl if j < CORES else wh, w3)[k][j % CORES if k == 2 else j]
            rows = u[span(behind(x, j) * SIDE + behind(y, k), fine), :]
            term = dot(w, rows, 1, 0)
            total = term if total is None else total + term
    rounded = total.astype(bf16)
    grad[...] = rounded
    entering(rounded, leading, c_rows, totals, states)


def scan_body(states, exits):
    count, size, _ = exits.shape
    held = jnp.zeros(exits.shape[1:], f32)
    for k in range(count - 1, -1, -1):
        exits[k] = held.astype(bf16)
        total = states[k, size : size + 16, :].astype(f32)
        held = (total[0:1] + total[1:2]) * held + states[k, :size, :].astype(f32)


def block_body(
    grad, leading, entry, leaving, b_cols, x_heads, kernel, mixed, gain, trailing, x_trailing, c_cols, out
):
    count = leading.shape[0]
    inner = grad.shape[0]
    each = inner // count
    size = b_cols.shape[0]
    scaled = []
    for h in range(count):
        own = slice(h * each, (h + 1) * each)
        scaled.append((grad[own, :].astype(f32) * leading[h : h + 1, :]).astype(bf16))
    grad_c = dot(entry[...], jnp.concatenate(scaled, axis=0), 1, 0)
    gained = dot(leaving[...], b_cols[...], 1, 0)
    weighted = None
    for h in range(count):
        own = slice(h * each, (h + 1) * each)
        g = grad[own, :]
        term = kernel[h].astype(f32) * dot(g, x_heads[own, :], 0, 0)
        weighted = term if weighted is None else weighted + term
        inside = dot(g, mixed[h], 1, 0) + gain[h : h + 1, :] * g.astype(f32)
        out[own, :] = (inside + trailing[h : h + 1, :] * gained[own, :]).astype(bf16)
    rounded = weighted.astype(bf16)
    grad_b = dot(c_cols[...], rounded, 1, 0) + dot(leaving[...], x_trailing[...], 0, 0)
    out[inner : inner + size, :] = grad_b.astype(bf16)
    out[inner + size :, :] = (grad_c + dot(b_cols[...], rounded, 1, 1)).astype(bf16)


def to_halves(u, q, core, keep, gives):
    share = keep.shape[1]
    keep[q] = u[span(core, share), :]
    part = share // len(gives)
    for i, give in enumerate(gives):
        give[q] = u[span((1 - core) * len(gives) + i, part), :]


def back_body(at, g0, g1, gl, gh, g3, w0, w1, wl, wh, w3, keep, give_a, give_b, u, g2):
    x, y, z, core = at[0], at[1], at[2], at[3]
    fine = w0.shape[0]
    g2[: gl.shape[0], :] = gl[...]
    g2[gl.shape[0] :, :] = gh[...]
    for k, g in enumerate((g0, g1, g2, g3)):
        for j, w in enumerate((w0, w1, None, w3)):
            rows = span(behind(y, j), fine)
            if w is None:
                term = jnp.concatenate([dot(wl[...], g[...], 1, 0), dot(wh[...], g[...], 1, 0)], axis=0)
            else:
                term = dot(w[...], g[...], 1, 0)
            u[k, rows, :] = term.astype(bf16)
        to_halves(u.at[k], z ^ x ^ behind(x, k), core, keep, (give_a, give_b))


def whole_body(at, g, w0, w1, wl, wh, w3, keep, give, u):
    x, y, z, core = at[0], at[1], at[2], at[3]
    fine = w0.shape[1]
    for k in range(SIDE):
        for j in range(SIDE):
            w = (w0, w1, wl if j < CORES else wh, w3)[k][j % CORES if k == 2 else j]
            u[k, span(behind(y, j), fine), :] = dot(w, g[...], 1, 0).astype(bf16)
        to_halves(u.at[k], z ^ behind(x, k), core, keep, (give,))


def rows_of(keep, q, got, part):
    size = got.shape[1]
    return keep[q, part * size : (part + 1) * size, :].astype(f32) + got[q].astype(f32)


def pair_body(part, keep, got, s1, s2, s3):
    for q, out in ((1, s1), (2, s2), (3, s3)):
        out[...] = rows_of(keep, q, got, part).astype(bf16)


def total_of(part, keep, got, received, upstream):
    total = rows_of(keep, 0, got, part)
    for r in received:
        total = total + r[...].astype(f32)
    return total + upstream.astype(f32)


def total_body(part, keep, got, r1, r2, r3, upstream, out):
    size = out.shape[0]
    own = upstream[part * size : (part + 1) * size, :]
    out[...] = total_of(part, keep, got, (r1, r2, r3), own).astype(bf16)


def result_body(at, keep, got, r1, r2, r3, upper, lower, settled, out):
    upstream = jnp.concatenate([upper[...], lower[...]], axis=0)
    total = total_of(0, keep, got, (r1, r2, r3), upstream).astype(bf16).astype(f32)
    chosen = jnp.where(at[4] == 1, settled[...].astype(f32), total)
    out[0] = chosen.T.astype(bf16)


def local(grad_out, w_out, w_in, w_bc, x_act, bc_act, decay, skip_gain, state_in):
    tie = lax.optimization_barrier
    section = lax.axis_index("section")
    ctx = lax.axis_index("ctx")
    heads_at = lax.axis_index("heads")
    x, y = ctx // SIDE, ctx % SIDE
    z, core = heads_at // CORES, heads_at % CORES
    at = jnp.stack([x, y, z, core, section]).astype(jnp.int32)
    rows, width = grad_out.shape
    block = width // SIDE
    share = block // CORES
    half = rows // CORES
    head_count, head_size, state_size = state_in.shape[2:]
    inner = head_count * head_size
    outer = inner + 2 * state_size
    pad = 16
    steps = (1, 2, 3)

    out_sides = sides(w_out[0], first_step, BOTH)
    out_far = far(out_sides, first_step, BOTH, 0)
    pieces = []
    for k in range(SIDE):
        low, count = (half * core, half) if k == 2 else (0, rows)
        pieces.append(lax.dynamic_slice(grad_out, (low, block * ((x + k) % SIDE)), (count, block)))
    own, *pieces = tie(pieces)
    before, across, after = [routed(p, along_x(k), (1,)) for k, p in zip(steps, pieces)]
    upstream = [own, before, across, routed(across, other_core, (1,)), after]

    back = jnp.concatenate([w_in[0], w_bc[0]], axis=1)
    out_far, back = tie((out_far, back))
    back_sides = sides(back, along_y, BOTH)

    (
        kernel, mixed, x_heads, x_trailing, entry, leading, trailing, totals, b_cols, c_cols, c_rows
    ) = call(
        tables_body,
        [
            struct((head_count, rows, rows)), struct((head_count, rows, rows)),
            struct((inner, rows)), struct((inner, rows)), struct((state_size, inner)),
            struct((head_count, rows), f32), struct((head_count, rows), f32),
            struct((head_count, pad, state_size)), struct((state_size, rows)),
            struct((state_size, rows)), struct((rows, state_size)),
        ],
        [decay[0], bc_act[0], x_act[0], state_in[0, 0]],
        remote=range(4),
        flops=2 * rows * rows * inner,
    )
    gain = jnp.broadcast_to(skip_gain[0][:, None], (head_count, rows))
    out_sides, out_far, leading, gain = tie((out_sides, out_far, leading, gain))

    state_shape = struct((head_count, head_size + pad, state_size))

    def exchange(states):
        return lax.all_to_all(states, "ctx", 0, 0)

    def scanned(arrived):
        (exits,) = call(
            scan_body, [struct((head_count, head_size, state_size))], [arrived], away=(0,)
        )
        return exits

    def within(grad_ssd, leaving, vmem_limit=VMEM):
        (grads,) = call(
            block_body,
            [struct((outer, rows))],
            [
                grad_ssd, leading, entry, leaving.reshape(inner, state_size), b_cols, x_heads, kernel, mixed,
                gain, trailing, x_trailing, c_cols,
            ],
            flops=4 * rows * rows * inner,
            remote=range(12),
            vmem_limit=vmem_limit,
        )
        return grads

    chunk = struct((share, rows))
    chunks = struct((SIDE, share, rows))

    def over_heads(keep, give, sections, part=0):
        got = routed(give, other_core, sections)
        sent = call(functools.partial(pair_body, part), [struct(give.shape[1:])] * 3, [keep, got])
        return [keep, got] + [routed(s, across_z(k), sections) for k, s in zip(steps, sent)]

    *partial, own = call(
        rows_body,
        [struct((inner, rows))] * SIDE + [chunk],
        [*upstream, out_sides[0], *out_far, out_sides[1], w_out[0]],
        at,
        remote=(9,),
        scratch=[pltpu.VMEM((SIDE, rows, block), bf16)],
        flops=2 * SIDE * rows * block * inner,
    )
    partial, out_sides, out_far = tie((partial, out_sides, out_far))
    received = [routed(partial[k], along_x(-k), (1,)) for k in steps]
    back_far = far(back_sides, along_y, BOTH, 0)
    out_set = jnp.concatenate([w_out[0], out_sides[0], *out_far, out_sides[1]]).reshape(SIDE, inner, -1)
    back_far, out_set = tie((back_far, out_set))
    whole_sides = sides(out_set, along_y, (0,))
    received, back_far = tie((received, back_far))
    back_set = jnp.concatenate([back, back_sides[0], *back_far, back_sides[1]]).reshape(SIDE, -1, outer)
    grad_ssd, states = call(
        sum_body,
        [struct((inner, rows)), state_shape],
        [partial[0], *received, leading, c_rows, totals],
        remote=(4, 5, 6),
        away=(0, 1),
        flops=2 * rows * inner * state_size,
    )

    states, back_set = tie((states, back_set))
    arrived = exchange(states)
    width_sides = sides(back_set, along_x, (0,))
    arrived, whole_sides, width_sides = tie((arrived, whole_sides, width_sides))
    exits = scanned(arrived)
    exits, whole_sides, width_sides = tie((exits, whole_sides, width_sides))
    leaving = exchange(exits)
    whole_far = far(whole_sides, along_y, (0,), 0)
    width_far = far(width_sides, along_x, (0,), 0)
    leaving, whole_far, width_far = tie((leaving, whole_far, width_far))
    grads = within(grad_ssd, leaving)

    grads_sides = sides(grads, along_x, (1,))
    grads_far = far(grads_sides, along_x, (1,), 0)
    wide = [pltpu.VMEM((SIDE, block, rows), bf16)]
    halves = struct((SIDE, share // 2, rows))
    keep, *gives = call(
        back_body,
        [chunks, halves, halves],
        [
            grads, grads_sides[0], *grads_far, grads_sides[1],
            back, back_sides[0], *back_far, back_sides[1],
        ],
        at,
        scratch=wide + [pltpu.VMEM((outer, rows), bf16)],
        flops=2 * SIDE * rows * block * outer,
    )
    middle = []
    for i, give in enumerate(gives):
        sums = over_heads(keep, give, (1,), i)
        middle += call(functools.partial(total_body, i), [struct((share // 2, rows))], [*sums, own])

    arrived = [routed(m, hop(0), (1,)) for m in middle]
    settled = routed(jnp.concatenate(middle), hop(None), (1,))

    parts = [[a] + [routed(a, across_z(k), (0,)) for k in steps] for a in arrived]
    others = [routed(jnp.stack(p), other_core, (0,)) for p in parts]
    grad_ssd, states = call(
        lower_body,
        [struct((inner, rows)), state_shape],
        [*parts[0], *parts[1], *others, out_set, whole_sides[0], *whole_far, whole_sides[1], leading, c_rows, totals],
        at,
        scratch=[pltpu.VMEM((width, rows), bf16)],
        remote=range(15, 18),
        away=(0, 1),
        flops=2 * rows * width * inner,
    )
    held, settled = tie((exchange(states), settled))
    grads = within(grad_ssd, exchange(scanned(held)), MOST)
    keep, give = call(
        whole_body,
        [chunks, chunks],
        [grads, back_set, width_sides[0], *width_far, width_sides[1]],
        at,
        scratch=wide,
        flops=2 * rows * width * outer,
    )
    sums = over_heads(keep, give, (0,))
    (result,) = call(result_body, [struct((1, rows, share))], [*sums, *arrived, settled], at)
    return result


def solution(mesh):
    placed = (
        P("ctx", None),
        P("section", "heads", "ctx"),
        P("section", "ctx", "heads"),
        P("section", "ctx", "heads"),
        P("section", "ctx", "heads"),
        P("section", "ctx", "heads"),
        P("section", "heads", "ctx"),
        P("section", "heads"),
        P("section", "ctx", "heads", None, None),
    )
    return jax.shard_map(
        local, mesh=mesh, in_specs=placed, out_specs=P("section", "ctx", "heads"), check_vma=False
    )
```

```python
import functools

import jax
import jax.numpy as jnp
from jax import lax
from jax.experimental import pallas as pl
from jax.experimental.pallas import tpu as pltpu
from jax.sharding import PartitionSpec as P

SIDE = 4
CORES = 2
BOTH = (0, 1)
AXES = ("section", "ctx", "heads")
ORDER = (2, 3, 1)
VMEM = 20 * 1024 * 1024
MOST = 54 * 1024 * 1024
bf16, f32 = jnp.bfloat16, jnp.float32


def place(section, x, y, z, core):
    return (((section * SIDE + x) * SIDE + y) * SIDE + z) * CORES + core


def routed(value, move, sections):
    pairs = []
    for section in sections:
        for x in range(SIDE):
            for y in range(SIDE):
                for z in range(SIDE):
                    for core in range(CORES):
                        here = (section, x, y, z, core)
                        pairs.append((place(*here), place(*move(*here))))
    return lax.ppermute(value, AXES, pairs)


def first_half(value, axis):
    return lax.slice_in_dim(value, 0, value.shape[axis] // 2, axis=axis)


def second_half(value, axis):
    return lax.slice_in_dim(value, value.shape[axis] // 2, value.shape[axis], axis=axis)


def sides(value, along, sections):
    return [routed(value, along(k), sections) for k in (1, 3)]


def far(both, along, sections, axis):
    before, after = both
    return [
        routed(first_half(before, axis), along(1), sections),
        routed(second_half(after, axis), along(3), sections),
    ]


def along_x(k):
    return lambda s, x, y, z, c: (s, (x + k) % SIDE, y, z, c)


def along_y(k):
    return lambda s, x, y, z, c: (s, x, (y + k) % SIDE, z, c)


def across_z(k):
    return lambda s, x, y, z, c: (s, x, y, z ^ k, c)


def other_core(s, x, y, z, c):
    return (s, x, y, z, 1 - c)


def hop(to_section):
    return lambda s, x, y, z, c: (s if to_section is None else to_section, x ^ z, y, x, c)


def first_step(k):
    return lambda s, x, y, z, c: (along_y if s == 1 else along_x)(k)(s, x, y, z, c)


def dot(left, right, left_dim, right_dim):
    return lax.dot_general(
        left, right, (((left_dim,), (right_dim,)), ((), ())), preferred_element_type=f32
    )


class Late:
    def __init__(self, source, held, sem):
        self.held, self.copy, self.waited = held, pltpu.make_async_copy(source, held, sem), False
        self.shape = held.shape

    def __getitem__(self, index):
        if not self.waited:
            self.copy.wait()
            self.waited = True
        return self.held[index]


def call(body, outs, args, at=None, scratch=(), flops=0, remote=(), away=(), aliases=(), vmem_limit=VMEM, where=None):
    moved = sum(a.size * a.dtype.itemsize for a in (*args, *outs))
    vmem, hbm = pl.BlockSpec(memory_space=pltpu.VMEM), pl.BlockSpec(memory_space=pltpu.HBM)
    own = [pltpu.VMEM(args[i].shape, args[i].dtype) for i in remote]
    own += [pltpu.VMEM(outs[i].shape, outs[i].dtype) for i in away]

    def run(refs):
        refs = list(refs)
        first = refs[:1] if at is not None else []
        refs = refs[len(first) :]
        ins, results = refs[: len(args)], refs[len(args) : len(args) + len(outs)]
        held = refs[len(args) + len(outs) :]
        sems = held.pop() if own else None
        held, extra = held[: len(own)], held[len(own) :]
        late = []
        for n, i in enumerate(remote):
            late.append(Late(ins[i], held[n], sems.at[n]))
            late[-1].copy.start()
            ins[i] = late[-1]
        targets = list(results)
        for n, i in enumerate(away):
            results[i] = held[len(remote) + n]
        body(*first, *ins, *results, *extra)
        for operand in late:
            if not operand.waited:
                operand[...]
        copies = [
            pltpu.make_async_copy(results[i], targets[i], sems.at[len(remote) + n])
            for n, i in enumerate(away)
        ]
        for copy in copies:
            copy.start()
        for copy in copies:
            copy.wait()

    def kernel(*refs):
        if where is None:
            run(refs)
        else:
            pl.when(refs[0][refs[0].shape[0] - 1] == where)(lambda: run(refs))

    return pl.pallas_call(
        kernel,
        in_specs=[pl.BlockSpec(memory_space=pltpu.SMEM)] * (at is not None)
        + [hbm if i in remote else vmem for i in range(len(args))],
        out_specs=[hbm if i in away else vmem for i in range(len(outs))],
        out_shape=list(outs),
        input_output_aliases=dict(aliases),
        scratch_shapes=own + list(scratch) + ([pltpu.SemaphoreType.DMA((len(own),))] if own else []),
        compiler_params=pltpu.CompilerParams(vmem_limit_bytes=vmem_limit),
        cost_estimate=pl.CostEstimate(flops=flops, bytes_accessed=moved, transcendentals=0),
    )(*([at] if at is not None else []), *args)


def struct(shape, dtype=bf16):
    return jax.ShapeDtypeStruct(shape, dtype)


def behind(index, k):
    return lax.rem(index + SIDE - k, SIDE)


def span(index, size):
    return pl.ds(pl.multiple_of(index * size, size), size)


def tables_body(
    decay, bc_rows, x_rows, state,
    kernel, mixed, x_heads, x_trailing, entry, leading, trailing, totals, b_cols, c_cols, c_rows,
):
    count, length = decay.shape
    size = b_cols.shape[0]
    each = x_heads.shape[0] // count
    exact = lax.Precision.HIGHEST
    earlier = lax.broadcasted_iota(jnp.int32, (length, length), 0)
    later = lax.broadcasted_iota(jnp.int32, (length, length), 1)
    lower = earlier >= later
    inner = (((1,), (0,)), ((), ()))
    last = (((1,), (1,)), ((), ()))
    rates = decay[...]
    sums = lax.dot_general(
        rates, (earlier <= later).astype(f32), inner, precision=exact, preferred_element_type=f32
    )
    columns = lax.dot_general(
        lower.astype(f32), rates, last, precision=exact, preferred_element_type=f32
    )
    b_part, c_part = bc_rows[:, :size], bc_rows[:, size:]
    common = dot(c_part, b_part, 1, 1)
    b_cols[...] = b_part.astype(f32).T.astype(bf16)
    c_cols[...] = c_part.astype(f32).T.astype(bf16)
    c_rows[...] = c_part
    lead = jnp.exp(sums)
    trail = jnp.exp(sums[:, length - 1 :] - sums)
    leading[...] = lead
    trailing[...] = trail
    first = lax.broadcasted_iota(jnp.int32, totals.shape[1:], 0) == 0
    for head in range(count):
        spread = columns[:, head : head + 1] - sums[head : head + 1, :]
        weights = jnp.where(lower, jnp.exp(jnp.minimum(spread, 0.0)), 0.0)
        kernel[head] = weights.astype(bf16)
        mixed[head] = (weights * common).astype(bf16)
        total = jnp.broadcast_to(lead[head : head + 1, length - 1 :], totals.shape[1:])
        high = total.astype(bf16).astype(f32)
        totals[head] = jnp.where(first, high, total - high).astype(bf16)
    for pair in range(count // 2):
        both = slice(pair * 2 * each, (pair + 1) * 2 * each)
        x_pair = x_rows[:, both].astype(f32).T
        x_heads[both, :] = x_pair.astype(bf16)
        for i in range(2):
            head = 2 * pair + i
            own = slice(head * each, (head + 1) * each)
            x_trailing[own, :] = (
                x_pair[i * each : (i + 1) * each, :] * trail[head : head + 1, :]
            ).astype(bf16)
        flat = jnp.concatenate([state[2 * pair], state[2 * pair + 1]], axis=0)
        entry[:, both] = flat.T.astype(bf16)


def rows_body(at, own, u1, u2, v2, u3, w1, wl, wh, w3, w0, o0, o1, o2, o3, piece, u):
    x, y, z, core = at[0], at[1], at[2], at[3]
    fine = w1.shape[1]
    half = u2.shape[0]
    u[0] = own[...]
    u[1] = u1[...]
    u[2, span(core, half), :] = u2[...]
    u[2, span(1 - core, half), :] = v2[...]
    u[3] = u3[...]
    piece[...] = u[behind(x, x ^ z), :, span(core, piece.shape[0])].astype(f32).T.astype(bf16)
    for k, out in enumerate((o0, o1, o2, o3)):
        total = None
        for j, w in enumerate((w0, w1, None, w3)):
            columns = u[k, :, span(behind(y, j), fine)]
            if w is None:
                term = jnp.concatenate([dot(wl[...], columns, 1, 1), dot(wh[...], columns, 1, 1)], axis=0)
            else:
                term = dot(w[...], columns, 1, 1)
            total = term if total is None else total + term
        out[...] = total.astype(bf16)


def entering(grad, leading, c_rows, totals, states):
    count = totals.shape[0]
    each = grad.shape[0] // count
    wide = grad.astype(f32)
    scaled = [
        (wide[h * each : (h + 1) * each] * leading[h : h + 1, :]).astype(bf16) for h in range(count)
    ]
    summed = dot(jnp.concatenate(scaled, axis=0), c_rows[...], 1, 0).astype(bf16)
    for h in range(count):
        states[h, :each, :] = summed[h * each : (h + 1) * each]
        states[h, each:, :] = totals[h]


def sum_body(own, r1, r2, r3, leading, c_rows, totals, grad, states):
    total = own[...].astype(f32)
    for r in (r1, r2, r3):
        total = total + r[...].astype(f32)
    rounded = total.astype(bf16)
    grad[...] = rounded
    entering(rounded, leading, c_rows, totals, states)


def lower_body(
    at, a0, a1, a2, a3, b0, b1, b2, b3, other_a, other_b, w0, w1, wl, wh, w3, leading, c_rows, totals, grad, states, u
):
    x, y, z, core = at[0], at[1], at[2], at[3]
    fine = a0.shape[0]
    for q in range(SIDE):
        base = (z ^ q) * CORES
        for i, (parts, other) in enumerate((((a0, a1, a2, a3), other_a), ((b0, b1, b2, b3), other_b))):
            u[span((base + core) * 2 + i, fine), :] = parts[q][...]
            u[span((base + 1 - core) * 2 + i, fine), :] = other[q]
    total = None
    for k in range(SIDE):
        for j in range(SIDE):
            w = (w0, w1, wl if j < CORES else wh, w3)[k][j % CORES if k == 2 else j]
            rows = u[span(behind(x, j) * SIDE + behind(y, k), fine), :]
            term = dot(w, rows, 1, 0)
            total = term if total is None else total + term
    rounded = total.astype(bf16)
    grad[...] = rounded
    entering(rounded, leading, c_rows, totals, states)


def scan_body(states, exits):
    count, size, _ = exits.shape
    held = jnp.zeros(exits.shape[1:], f32)
    for k in range(count - 1, -1, -1):
        exits[k] = held.astype(bf16)
        total = states[k, size : size + 16, :].astype(f32)
        held = (total[0:1] + total[1:2]) * held + states[k, :size, :].astype(f32)


def block_body(
    grad, leading, entry, leaving, b_cols, x_heads, kernel, mixed, gain, trailing, x_trailing, c_cols, out
):
    count = leading.shape[0]
    inner = grad.shape[0]
    each = inner // count
    size = b_cols.shape[0]
    scaled = []
    for h in range(count):
        own = slice(h * each, (h + 1) * each)
        scaled.append((grad[own, :].astype(f32) * leading[h : h + 1, :]).astype(bf16))
    grad_c = dot(entry[...], jnp.concatenate(scaled, axis=0), 1, 0)
    gained = dot(leaving[...], b_cols[...], 1, 0)
    weighted = None
    for h in range(count):
        own = slice(h * each, (h + 1) * each)
        g = grad[own, :]
        term = kernel[h].astype(f32) * dot(g, x_heads[own, :], 0, 0)
        weighted = term if weighted is None else weighted + term
        inside = dot(g, mixed[h], 1, 0) + gain[h : h + 1, :] * g.astype(f32)
        out[own, :] = (inside + trailing[h : h + 1, :] * gained[own, :]).astype(bf16)
    rounded = weighted.astype(bf16)
    grad_b = dot(c_cols[...], rounded, 1, 0) + dot(leaving[...], x_trailing[...], 0, 0)
    out[inner : inner + size, :] = grad_b.astype(bf16)
    out[inner + size :, :] = (grad_c + dot(b_cols[...], rounded, 1, 1)).astype(bf16)


def to_halves(u, q, core, keep, gives):
    share = keep.shape[1]
    keep[q] = u[span(core, share), :]
    part = share // len(gives)
    for i, give in enumerate(gives):
        give[q] = u[span((1 - core) * len(gives) + i, part), :]


def block_terms(at, g, weights, u):
    for j, w in enumerate(weights):
        rows = span(behind(at[1], j), u.shape[0] // SIDE)
        term = [dot(part[...], g[...], 1, 0) for part in w]
        u[rows, :] = jnp.concatenate(term, axis=0).astype(bf16)


def near_body(at, g0, g1, g3, w0, w1, wl, wh, w3, keep, give_a, give_b, u):
    x, z, core = at[0], at[2], at[3]
    for k, g in ((0, g0), (1, g1), (3, g3)):
        block_terms(at, g, ((w0,), (w1,), (wl, wh), (w3,)), u.at[k])
        to_halves(u.at[k], z ^ x ^ behind(x, k), core, keep, (give_a, give_b))


def far_body(at, gl, gh, w0, w1, wl, wh, w3, k0, k1, k2, keep, give_a, give_b, u, g):
    x, z, core = at[0], at[2], at[3]
    g[: gl.shape[0], :] = gl[...]
    g[gl.shape[0] :, :] = gh[...]
    block_terms(at, g, ((w0,), (w1,), (wl, wh), (w3,)), u)
    to_halves(u, z ^ x ^ behind(x, 2), core, keep, (give_a, give_b))


def whole_body(at, g, w0, w1, wl, wh, w3, keep, give, u):
    x, y, z, core = at[0], at[1], at[2], at[3]
    fine = w0.shape[1]
    for k in range(SIDE):
        for j in range(SIDE):
            w = (w0, w1, wl if j < CORES else wh, w3)[k][j % CORES if k == 2 else j]
            u[k, span(behind(y, j), fine), :] = dot(w, g[...], 1, 0).astype(bf16)
        to_halves(u.at[k], z ^ behind(x, k), core, keep, (give,))


def rows_of(keep, q, got, part):
    size = got.shape[1]
    return keep[q, part * size : (part + 1) * size, :].astype(f32) + got[q].astype(f32)


def pair_body(part, keep, got, s1, s2, s3):
    for q, out in zip(ORDER, (s1, s2, s3)):
        out[...] = rows_of(keep, q, got, part).astype(bf16)


def total_of(part, keep, got, received, upstream):
    total = rows_of(keep, 0, got, part)
    for r in received:
        total = total + r[...].astype(f32)
    return total + upstream.astype(f32)


def total_body(part, keep, got, r1, r2, r3, upstream, out):
    size = out.shape[0]
    own = upstream[part * size : (part + 1) * size, :]
    out[...] = total_of(part, keep, got, (r1, r2, r3), own).astype(bf16)


def result_body(at, keep, got, r1, r2, r3, upper, lower, settled, out):
    upstream = jnp.concatenate([upper[...], lower[...]], axis=0)
    total = total_of(0, keep, got, (r1, r2, r3), upstream).astype(bf16).astype(f32)
    chosen = jnp.where(at[4] == 1, settled[...].astype(f32), total)
    out[0] = chosen.T.astype(bf16)


def local(grad_out, w_out, w_in, w_bc, x_act, bc_act, decay, skip_gain, state_in):
    tie = lax.optimization_barrier
    section = lax.axis_index("section")
    ctx = lax.axis_index("ctx")
    heads_at = lax.axis_index("heads")
    x, y = ctx // SIDE, ctx % SIDE
    z, core = heads_at // CORES, heads_at % CORES
    at = jnp.stack([x, y, z, core, section]).astype(jnp.int32)
    rows, width = grad_out.shape
    block = width // SIDE
    share = block // CORES
    half = rows // CORES
    head_count, head_size, state_size = state_in.shape[2:]
    inner = head_count * head_size
    outer = inner + 2 * state_size
    pad = 16
    steps = (1, 2, 3)

    out_sides = sides(w_out[0], first_step, BOTH)
    out_far = far(out_sides, first_step, BOTH, 0)
    pieces = []
    for k in range(SIDE):
        low, count = (half * core, half) if k == 2 else (0, rows)
        pieces.append(lax.dynamic_slice(grad_out, (low, block * ((x + k) % SIDE)), (count, block)))
    own, *pieces = pieces
    pieces = tie(pieces)
    before, across, after = [routed(p, along_x(k), (1,)) for k, p in zip(steps, pieces)]
    upstream = [own, before, across, routed(across, other_core, (1,)), after]

    back = jnp.concatenate([w_in[0], w_bc[0]], axis=1)
    out_far, back = tie((out_far, back))
    back_sides = sides(back, along_y, BOTH)

    (
        kernel, mixed, x_heads, x_trailing, entry, leading, trailing, totals, b_cols, c_cols, c_rows
    ) = call(
        tables_body,
        [
            struct((head_count, rows, rows)), struct((head_count, rows, rows)),
            struct((inner, rows)), struct((inner, rows)), struct((state_size, inner)),
            struct((head_count, rows), f32), struct((head_count, rows), f32),
            struct((head_count, pad, state_size)), struct((state_size, rows)),
            struct((state_size, rows)), struct((rows, state_size)),
        ],
        [decay[0], bc_act[0], x_act[0], state_in[0, 0]],
        remote=range(4),
        flops=2 * rows * rows * inner,
    )
    gain = jnp.broadcast_to(skip_gain[0][:, None], (head_count, rows))
    out_sides, out_far, leading, gain = tie((out_sides, out_far, leading, gain))

    state_shape = struct((head_count, head_size + pad, state_size))

    def exchange(states):
        return lax.all_to_all(states, "ctx", 0, 0)

    def scanned(arrived):
        (exits,) = call(
            scan_body, [struct((head_count, head_size, state_size))], [arrived], away=(0,)
        )
        return exits

    def within(grad_ssd, leaving, vmem_limit=VMEM):
        (grads,) = call(
            block_body,
            [struct((outer, rows))],
            [
                grad_ssd, leading, entry, leaving.reshape(inner, state_size), b_cols, x_heads, kernel, mixed,
                gain, trailing, x_trailing, c_cols,
            ],
            flops=4 * rows * rows * inner,
            remote=range(12),
            vmem_limit=vmem_limit,
        )
        return grads

    chunk = struct((share, rows))
    chunks = struct((SIDE, share, rows))

    def over_heads(keep, give, sections, part=0):
        got = routed(give, other_core, sections)
        sent = call(functools.partial(pair_body, part), [struct(give.shape[1:])] * 3, [keep, got])
        return [keep, got] + [routed(s, across_z(k), sections) for k, s in zip(ORDER, sent)]

    *partial, own = call(
        rows_body,
        [struct((inner, rows))] * SIDE + [chunk],
        [*upstream, out_sides[0], *out_far, out_sides[1], w_out[0]],
        at,
        remote=(9,),
        scratch=[pltpu.VMEM((SIDE, rows, block), bf16)],
        flops=2 * SIDE * rows * block * inner,
        where=1,
    )
    partial, out_sides, out_far = tie((partial, out_sides, out_far))
    received = [routed(partial[k], along_x(-k), (1,)) for k in steps]
    back_far = far(back_sides, along_y, BOTH, 0)
    out_set = jnp.concatenate([w_out[0], out_sides[0], *out_far, out_sides[1]]).reshape(SIDE, inner, -1)
    back_far, out_set = tie((back_far, out_set))
    whole_sides = sides(out_set, along_y, (0,))
    received, back_far = tie((received, back_far))
    back_set = jnp.concatenate([back, back_sides[0], *back_far, back_sides[1]]).reshape(SIDE, -1, outer)
    grad_ssd, states = call(
        sum_body,
        [struct((inner, rows)), state_shape],
        [partial[0], *received, leading, c_rows, totals],
        remote=(4, 5, 6),
        away=(0, 1),
        flops=2 * rows * inner * state_size,
    )

    states, back_set = tie((states, back_set))
    arrived = exchange(states)
    width_sides = sides(back_set, along_x, (0,))
    arrived, whole_sides, width_sides = tie((arrived, whole_sides, width_sides))
    exits = scanned(arrived)
    exits, whole_sides, width_sides = tie((exits, whole_sides, width_sides))
    leaving = exchange(exits)
    whole_far = far(whole_sides, along_y, (0,), 0)
    width_far = far(width_sides, along_x, (0,), 0)
    leaving, whole_far, width_far = tie((leaving, whole_far, width_far))
    grads = within(grad_ssd, leaving)

    grads_sides = sides(grads, along_x, (1,))
    grads_far = far(grads_sides, along_x, (1,), 0)
    wide = [pltpu.VMEM((SIDE, block, rows), bf16)]
    halves = struct((SIDE, share // 2, rows))
    weights = [back, back_sides[0], *back_far, back_sides[1]]
    first = call(
        near_body,
        [chunks, halves, halves],
        [grads, *grads_sides, *weights],
        at,
        scratch=wide,
        flops=6 * rows * block * outer,
        where=1,
    )
    keep, *gives = call(
        far_body,
        [chunks, halves, halves],
        [*grads_far, *weights, *first],
        at,
        scratch=[pltpu.VMEM((block, rows), bf16), pltpu.VMEM((outer, rows), bf16)],
        flops=2 * rows * block * outer,
        aliases={8: 0, 9: 1, 10: 2},
        where=1,
    )

    middle = []
    for i, give in enumerate(gives):
        sums = over_heads(keep, give, (1,), i)
        middle += call(functools.partial(total_body, i), [struct((share // 2, rows))], [*sums, own])

    arrived = [routed(m, hop(0), (1,)) for m in middle]
    settled = routed(jnp.concatenate(middle), hop(None), (1,))

    parts = [[a] + [routed(a, across_z(k), (0,)) for k in steps] for a in arrived]
    others = [routed(jnp.stack(p), other_core, (0,)) for p in parts]
    grad_ssd, states = call(
        lower_body,
        [struct((inner, rows)), state_shape],
        [*parts[0], *parts[1], *others, out_set, whole_sides[0], *whole_far, whole_sides[1], leading, c_rows, totals],
        at,
        scratch=[pltpu.VMEM((width, rows), bf16)],
        remote=range(15, 18),
        away=(0, 1),
        flops=2 * rows * width * inner,
    )
    held, settled = tie((exchange(states), settled))
    grads = within(grad_ssd, exchange(scanned(held)), MOST)
    keep, give = call(
        whole_body,
        [chunks, chunks],
        [grads, back_set, width_sides[0], *width_far, width_sides[1]],
        at,
        scratch=wide,
        flops=2 * rows * width * outer,
    )
    sums = over_heads(keep, give, (0,))
    (result,) = call(result_body, [struct((1, rows, share))], [*sums, *arrived, settled], at)
    return result


def solution(mesh):
    placed = (
        P("ctx", None),
        P("section", "heads", "ctx"),
        P("section", "ctx", "heads"),
        P("section", "ctx", "heads"),
        P("section", "ctx", "heads"),
        P("section", "ctx", "heads"),
        P("section", "heads", "ctx"),
        P("section", "heads"),
        P("section", "ctx", "heads", None, None),
    )
    return jax.shard_map(
        local, mesh=mesh, in_specs=placed, out_specs=P("section", "ctx", "heads"), check_vma=False
    )
```

```python
import functools

import jax
import jax.numpy as jnp
from jax import lax
from jax.experimental import pallas as pl
from jax.experimental.pallas import tpu as pltpu
from jax.sharding import PartitionSpec as P

SIDE = 4
CORES = 2
BOTH = (0, 1)
AXES = ("section", "ctx", "heads")
MIDDLE_FIRST, IN_TURN = (2, 3, 1), (1, 2, 3)
VMEM = 20 * 1024 * 1024
MOST = 54 * 1024 * 1024
bf16, f32 = jnp.bfloat16, jnp.float32


def place(section, x, y, z, core):
    return (((section * SIDE + x) * SIDE + y) * SIDE + z) * CORES + core


def routed(value, move, sections):
    pairs = []
    for section in sections:
        for x in range(SIDE):
            for y in range(SIDE):
                for z in range(SIDE):
                    for core in range(CORES):
                        here = (section, x, y, z, core)
                        pairs.append((place(*here), place(*move(*here))))
    return lax.ppermute(value, AXES, pairs)


def first_half(value, axis):
    return lax.slice_in_dim(value, 0, value.shape[axis] // 2, axis=axis)


def second_half(value, axis):
    return lax.slice_in_dim(value, value.shape[axis] // 2, value.shape[axis], axis=axis)


def sides(value, along, sections):
    return [routed(value, along(k), sections) for k in (1, 3)]


def far(both, along, sections, axis):
    before, after = both
    return [
        routed(first_half(before, axis), along(1), sections),
        routed(second_half(after, axis), along(3), sections),
    ]


def along_x(k):
    return lambda s, x, y, z, c: (s, (x + k) % SIDE, y, z, c)


def along_y(k):
    return lambda s, x, y, z, c: (s, x, (y + k) % SIDE, z, c)


def across_z(k):
    return lambda s, x, y, z, c: (s, x, y, z ^ k, c)


def other_core(s, x, y, z, c):
    return (s, x, y, z, 1 - c)


def hop(to_section):
    return lambda s, x, y, z, c: (s if to_section is None else to_section, x ^ z, y, x, c)


def first_step(k):
    return lambda s, x, y, z, c: (along_y if s == 1 else along_x)(k)(s, x, y, z, c)


def dot(left, right, left_dim, right_dim):
    return lax.dot_general(
        left, right, (((left_dim,), (right_dim,)), ((), ())), preferred_element_type=f32
    )


class Late:
    def __init__(self, source, held, sem):
        self.held, self.copy, self.waited = held, pltpu.make_async_copy(source, held, sem), False
        self.shape = held.shape

    def __getitem__(self, index):
        if not self.waited:
            self.copy.wait()
            self.waited = True
        return self.held[index]


def call(body, outs, args, at=None, scratch=(), flops=0, remote=(), away=(), aliases=(), vmem_limit=VMEM, where=None):
    moved = sum(a.size * a.dtype.itemsize for a in (*args, *outs))
    vmem, hbm = pl.BlockSpec(memory_space=pltpu.VMEM), pl.BlockSpec(memory_space=pltpu.HBM)
    own = [pltpu.VMEM(args[i].shape, args[i].dtype) for i in remote]
    own += [pltpu.VMEM(outs[i].shape, outs[i].dtype) for i in away]

    def run(refs):
        refs = list(refs)
        first = refs[:1] if at is not None else []
        refs = refs[len(first) :]
        ins, results = refs[: len(args)], refs[len(args) : len(args) + len(outs)]
        held = refs[len(args) + len(outs) :]
        sems = held.pop() if own else None
        held, extra = held[: len(own)], held[len(own) :]
        late = []
        for n, i in enumerate(remote):
            late.append(Late(ins[i], held[n], sems.at[n]))
            late[-1].copy.start()
            ins[i] = late[-1]
        targets = list(results)
        for n, i in enumerate(away):
            results[i] = held[len(remote) + n]
        body(*first, *ins, *results, *extra)
        for operand in late:
            if not operand.waited:
                operand[...]
        copies = [
            pltpu.make_async_copy(results[i], targets[i], sems.at[len(remote) + n])
            for n, i in enumerate(away)
        ]
        for copy in copies:
            copy.start()
        for copy in copies:
            copy.wait()

    def kernel(*refs):
        if where is None:
            run(refs)
        else:
            pl.when(refs[0][refs[0].shape[0] - 1] == where)(lambda: run(refs))

    return pl.pallas_call(
        kernel,
        in_specs=[pl.BlockSpec(memory_space=pltpu.SMEM)] * (at is not None)
        + [hbm if i in remote else vmem for i in range(len(args))],
        out_specs=[hbm if i in away else vmem for i in range(len(outs))],
        out_shape=list(outs),
        input_output_aliases=dict(aliases),
        scratch_shapes=own + list(scratch) + ([pltpu.SemaphoreType.DMA((len(own),))] if own else []),
        compiler_params=pltpu.CompilerParams(vmem_limit_bytes=vmem_limit),
        cost_estimate=pl.CostEstimate(flops=flops, bytes_accessed=moved, transcendentals=0),
    )(*([at] if at is not None else []), *args)


def struct(shape, dtype=bf16):
    return jax.ShapeDtypeStruct(shape, dtype)


def behind(index, k):
    return lax.rem(index + SIDE - k, SIDE)


def span(index, size):
    return pl.ds(pl.multiple_of(index * size, size), size)


def tables_body(
    decay, bc_rows, x_rows, state,
    kernel, mixed, x_heads, x_trailing, entry, leading, trailing, totals, b_cols, c_cols, c_rows,
):
    count, length = decay.shape
    size = b_cols.shape[0]
    each = x_heads.shape[0] // count
    exact = lax.Precision.HIGHEST
    earlier = lax.broadcasted_iota(jnp.int32, (length, length), 0)
    later = lax.broadcasted_iota(jnp.int32, (length, length), 1)
    lower = earlier >= later
    inner = (((1,), (0,)), ((), ()))
    last = (((1,), (1,)), ((), ()))
    rates = decay[...]
    sums = lax.dot_general(
        rates, (earlier <= later).astype(f32), inner, precision=exact, preferred_element_type=f32
    )
    columns = lax.dot_general(
        lower.astype(f32), rates, last, precision=exact, preferred_element_type=f32
    )
    b_part, c_part = bc_rows[:, :size], bc_rows[:, size:]
    common = dot(c_part, b_part, 1, 1)
    b_cols[...] = b_part.astype(f32).T.astype(bf16)
    c_cols[...] = c_part.astype(f32).T.astype(bf16)
    c_rows[...] = c_part
    lead = jnp.exp(sums)
    trail = jnp.exp(sums[:, length - 1 :] - sums)
    leading[...] = lead
    trailing[...] = trail
    first = lax.broadcasted_iota(jnp.int32, totals.shape[1:], 0) == 0
    for head in range(count):
        spread = columns[:, head : head + 1] - sums[head : head + 1, :]
        weights = jnp.where(lower, jnp.exp(jnp.minimum(spread, 0.0)), 0.0)
        kernel[head] = weights.astype(bf16)
        mixed[head] = (weights * common).astype(bf16)
        total = jnp.broadcast_to(lead[head : head + 1, length - 1 :], totals.shape[1:])
        high = total.astype(bf16).astype(f32)
        totals[head] = jnp.where(first, high, total - high).astype(bf16)
    for pair in range(count // 2):
        both = slice(pair * 2 * each, (pair + 1) * 2 * each)
        x_pair = x_rows[:, both].astype(f32).T
        x_heads[both, :] = x_pair.astype(bf16)
        for i in range(2):
            head = 2 * pair + i
            own = slice(head * each, (head + 1) * each)
            x_trailing[own, :] = (
                x_pair[i * each : (i + 1) * each, :] * trail[head : head + 1, :]
            ).astype(bf16)
        flat = jnp.concatenate([state[2 * pair], state[2 * pair + 1]], axis=0)
        entry[:, both] = flat.T.astype(bf16)


def rows_body(at, own, u1, u2, v2, u3, w1, wl, wh, w3, w0, o0, o1, o2, o3, piece, u):
    x, y, z, core = at[0], at[1], at[2], at[3]
    fine = w1.shape[1]
    half = u2.shape[0]
    u[0] = own[...]
    u[1] = u1[...]
    u[2, span(core, half), :] = u2[...]
    u[2, span(1 - core, half), :] = v2[...]
    u[3] = u3[...]
    piece[...] = u[behind(x, x ^ z), :, span(core, piece.shape[0])].astype(f32).T.astype(bf16)
    for k, out in enumerate((o0, o1, o2, o3)):
        total = None
        for j, w in enumerate((w0, w1, None, w3)):
            columns = u[k, :, span(behind(y, j), fine)]
            if w is None:
                term = jnp.concatenate([dot(wl[...], columns, 1, 1), dot(wh[...], columns, 1, 1)], axis=0)
            else:
                term = dot(w[...], columns, 1, 1)
            total = term if total is None else total + term
        out[...] = total.astype(bf16)


def entering(grad, leading, c_rows, totals, states):
    count = totals.shape[0]
    each = grad.shape[0] // count
    wide = grad.astype(f32)
    scaled = [
        (wide[h * each : (h + 1) * each] * leading[h : h + 1, :]).astype(bf16) for h in range(count)
    ]
    summed = dot(jnp.concatenate(scaled, axis=0), c_rows[...], 1, 0).astype(bf16)
    for h in range(count):
        states[h, :each, :] = summed[h * each : (h + 1) * each]
        states[h, each:, :] = totals[h]


def sum_body(own, r1, r2, r3, leading, c_rows, totals, grad, states):
    total = own[...].astype(f32)
    for r in (r1, r2, r3):
        total = total + r[...].astype(f32)
    rounded = total.astype(bf16)
    grad[...] = rounded
    entering(rounded, leading, c_rows, totals, states)


def lower_body(
    at, a0, a1, a2, a3, b0, b1, b2, b3, other_a, other_b, w0, w1, wl, wh, w3, leading, c_rows, totals, grad, states, u
):
    x, y, z, core = at[0], at[1], at[2], at[3]
    fine = a0.shape[0]
    for q in range(SIDE):
        base = (z ^ q) * CORES
        for i, (parts, other) in enumerate((((a0, a1, a2, a3), other_a), ((b0, b1, b2, b3), other_b))):
            u[span((base + core) * 2 + i, fine), :] = parts[q][...]
            u[span((base + 1 - core) * 2 + i, fine), :] = other[q]
    total = None
    for k in range(SIDE):
        for j in range(SIDE):
            w = (w0, w1, wl if j < CORES else wh, w3)[k][j % CORES if k == 2 else j]
            rows = u[span(behind(x, j) * SIDE + behind(y, k), fine), :]
            term = dot(w, rows, 1, 0)
            total = term if total is None else total + term
    rounded = total.astype(bf16)
    grad[...] = rounded
    entering(rounded, leading, c_rows, totals, states)


def scan_body(states, exits):
    count, size, _ = exits.shape
    held = jnp.zeros(exits.shape[1:], f32)
    for k in range(count - 1, -1, -1):
        exits[k] = held.astype(bf16)
        total = states[k, size : size + 16, :].astype(f32)
        held = (total[0:1] + total[1:2]) * held + states[k, :size, :].astype(f32)


def block_body(
    grad, leading, entry, leaving, b_cols, x_heads, kernel, mixed, gain, trailing, x_trailing, c_cols, out
):
    count = leading.shape[0]
    inner = grad.shape[0]
    each = inner // count
    size = b_cols.shape[0]
    scaled = []
    for h in range(count):
        own = slice(h * each, (h + 1) * each)
        scaled.append((grad[own, :].astype(f32) * leading[h : h + 1, :]).astype(bf16))
    grad_c = dot(entry[...], jnp.concatenate(scaled, axis=0), 1, 0)
    gained = dot(leaving[...], b_cols[...], 1, 0)
    weighted = None
    for h in range(count):
        own = slice(h * each, (h + 1) * each)
        g = grad[own, :]
        term = kernel[h].astype(f32) * dot(g, x_heads[own, :], 0, 0)
        weighted = term if weighted is None else weighted + term
        inside = dot(g, mixed[h], 1, 0) + gain[h : h + 1, :] * g.astype(f32)
        out[own, :] = (inside + trailing[h : h + 1, :] * gained[own, :]).astype(bf16)
    rounded = weighted.astype(bf16)
    grad_b = dot(c_cols[...], rounded, 1, 0) + dot(leaving[...], x_trailing[...], 0, 0)
    out[inner : inner + size, :] = grad_b.astype(bf16)
    out[inner + size :, :] = (grad_c + dot(b_cols[...], rounded, 1, 1)).astype(bf16)


def to_halves(u, q, core, keep, gives):
    share = keep.shape[1]
    keep[q] = u[span(core, share), :]
    part = share // len(gives)
    for i, give in enumerate(gives):
        give[q] = u[span((1 - core) * len(gives) + i, part), :]


def block_terms(at, g, weights, u):
    for j, w in enumerate(weights):
        rows = span(behind(at[1], j), u.shape[0] // SIDE)
        term = [dot(part[...], g[...], 1, 0) for part in w]
        u[rows, :] = jnp.concatenate(term, axis=0).astype(bf16)


def near_body(at, g0, g1, g3, w0, w1, wl, wh, w3, keep, give_a, give_b, u):
    x, z, core = at[0], at[2], at[3]
    for k, g in ((0, g0), (1, g1), (3, g3)):
        block_terms(at, g, ((w0,), (w1,), (wl, wh), (w3,)), u.at[k])
        to_halves(u.at[k], z ^ x ^ behind(x, k), core, keep, (give_a, give_b))


def far_body(at, gl, gh, w0, w1, wl, wh, w3, k0, k1, k2, keep, give_a, give_b, u, g):
    x, z, core = at[0], at[2], at[3]
    g[: gl.shape[0], :] = gl[...]
    g[gl.shape[0] :, :] = gh[...]
    block_terms(at, g, ((w0,), (w1,), (wl, wh), (w3,)), u)
    to_halves(u, z ^ x ^ behind(x, 2), core, keep, (give_a, give_b))


def whole_body(at, g, w0, w1, wl, wh, w3, keep, give, u):
    x, y, z, core = at[0], at[1], at[2], at[3]
    fine = w0.shape[1]
    for k in range(SIDE):
        for j in range(SIDE):
            w = (w0, w1, wl if j < CORES else wh, w3)[k][j % CORES if k == 2 else j]
            u[k, span(behind(y, j), fine), :] = dot(w, g[...], 1, 0).astype(bf16)
        to_halves(u.at[k], z ^ behind(x, k), core, keep, (give,))


def rows_of(keep, q, got, part):
    size = got.shape[1]
    return keep[q, part * size : (part + 1) * size, :].astype(f32) + got[q].astype(f32)


def pair_body(order, part, keep, got, s1, s2, s3):
    for q, out in zip(order, (s1, s2, s3)):
        out[...] = rows_of(keep, q, got, part).astype(bf16)


def total_of(part, keep, got, received, upstream):
    total = rows_of(keep, 0, got, part)
    for r in received:
        total = total + r[...].astype(f32)
    return total + upstream.astype(f32)


def total_body(part, keep, got, r1, r2, r3, upstream, out):
    size = out.shape[0]
    own = upstream[part * size : (part + 1) * size, :]
    out[...] = total_of(part, keep, got, (r1, r2, r3), own).astype(bf16)


def result_body(at, keep, got, r1, r2, r3, upper, lower, settled, out):
    upstream = jnp.concatenate([upper[...], lower[...]], axis=0)
    total = total_of(0, keep, got, (r1, r2, r3), upstream).astype(bf16).astype(f32)
    chosen = jnp.where(at[4] == 1, settled[...].astype(f32), total)
    out[0] = chosen.T.astype(bf16)


def local(grad_out, w_out, w_in, w_bc, x_act, bc_act, decay, skip_gain, state_in):
    tie = lax.optimization_barrier
    section = lax.axis_index("section")
    ctx = lax.axis_index("ctx")
    heads_at = lax.axis_index("heads")
    x, y = ctx // SIDE, ctx % SIDE
    z, core = heads_at // CORES, heads_at % CORES
    at = jnp.stack([x, y, z, core, section]).astype(jnp.int32)
    rows, width = grad_out.shape
    block = width // SIDE
    share = block // CORES
    half = rows // CORES
    head_count, head_size, state_size = state_in.shape[2:]
    inner = head_count * head_size
    outer = inner + 2 * state_size
    pad = 16
    steps = (1, 2, 3)

    out_sides = sides(w_out[0], first_step, BOTH)
    out_far = far(out_sides, first_step, BOTH, 0)
    pieces = []
    for k in range(SIDE):
        low, count = (half * core, half) if k == 2 else (0, rows)
        pieces.append(lax.dynamic_slice(grad_out, (low, block * ((x + k) % SIDE)), (count, block)))
    own, *pieces = pieces
    pieces = tie(pieces)
    before, across, after = [routed(p, along_x(k), (1,)) for k, p in zip(steps, pieces)]
    upstream = [own, before, across, routed(across, other_core, (1,)), after]

    back = jnp.concatenate([w_in[0], w_bc[0]], axis=1)
    out_far, back = tie((out_far, back))
    back_sides = sides(back, along_y, BOTH)

    (
        kernel, mixed, x_heads, x_trailing, entry, leading, trailing, totals, b_cols, c_cols, c_rows
    ) = call(
        tables_body,
        [
            struct((head_count, rows, rows)), struct((head_count, rows, rows)),
            struct((inner, rows)), struct((inner, rows)), struct((state_size, inner)),
            struct((head_count, rows), f32), struct((head_count, rows), f32),
            struct((head_count, pad, state_size)), struct((state_size, rows)),
            struct((state_size, rows)), struct((rows, state_size)),
        ],
        [decay[0], bc_act[0], x_act[0], state_in[0, 0]],
        remote=range(4),
        flops=2 * rows * rows * inner,
    )
    gain = jnp.broadcast_to(skip_gain[0][:, None], (head_count, rows))
    out_sides, out_far, leading, gain = tie((out_sides, out_far, leading, gain))

    state_shape = struct((head_count, head_size + pad, state_size))

    def exchange(states):
        return lax.all_to_all(states, "ctx", 0, 0)

    def scanned(arrived):
        (exits,) = call(
            scan_body, [struct((head_count, head_size, state_size))], [arrived], away=(0,)
        )
        return exits

    def within(grad_ssd, leaving, vmem_limit=VMEM):
        (grads,) = call(
            block_body,
            [struct((outer, rows))],
            [
                grad_ssd, leading, entry, leaving.reshape(inner, state_size), b_cols, x_heads, kernel, mixed,
                gain, trailing, x_trailing, c_cols,
            ],
            flops=4 * rows * rows * inner,
            remote=range(12),
            vmem_limit=vmem_limit,
        )
        return grads

    chunk = struct((share, rows))
    chunks = struct((SIDE, share, rows))

    def over_heads(keep, give, sections, order, part=0):
        got = routed(give, other_core, sections)
        sent = call(functools.partial(pair_body, order, part), [struct(give.shape[1:])] * 3, [keep, got])
        return [keep, got] + [routed(s, across_z(k), sections) for k, s in zip(order, sent)]

    *partial, own = call(
        rows_body,
        [struct((inner, rows))] * SIDE + [chunk],
        [*upstream, out_sides[0], *out_far, out_sides[1], w_out[0]],
        at,
        remote=(9,),
        scratch=[pltpu.VMEM((SIDE, rows, block), bf16)],
        flops=2 * SIDE * rows * block * inner,
        where=1,
    )
    partial, out_sides, out_far = tie((partial, out_sides, out_far))
    received = [routed(partial[k], along_x(-k), (1,)) for k in steps]
    back_far = far(back_sides, along_y, BOTH, 0)
    out_set = jnp.concatenate([w_out[0], out_sides[0], *out_far, out_sides[1]]).reshape(SIDE, inner, -1)
    back_far, out_set = tie((back_far, out_set))
    whole_sides = sides(out_set, along_y, (0,))
    received, back_far = tie((received, back_far))
    back_set = jnp.concatenate([back, back_sides[0], *back_far, back_sides[1]]).reshape(SIDE, -1, outer)
    grad_ssd, states = call(
        sum_body,
        [struct((inner, rows)), state_shape],
        [partial[0], *received, leading, c_rows, totals],
        remote=(4, 5, 6),
        away=(0, 1),
        flops=2 * rows * inner * state_size,
    )

    states, back_set = tie((states, back_set))
    arrived = exchange(states)
    width_sides = sides(back_set, along_x, (0,))
    arrived, whole_sides, width_sides = tie((arrived, whole_sides, width_sides))
    exits = scanned(arrived)
    exits, whole_sides, width_sides = tie((exits, whole_sides, width_sides))
    leaving = exchange(exits)
    whole_far = far(whole_sides, along_y, (0,), 0)
    width_far = far(width_sides, along_x, (0,), 0)
    leaving, whole_far, width_far = tie((leaving, whole_far, width_far))
    grads = within(grad_ssd, leaving)

    grads_sides = sides(grads, along_x, (1,))
    grads_far = far(grads_sides, along_x, (1,), 0)
    wide = [pltpu.VMEM((SIDE, block, rows), bf16)]
    halves = struct((SIDE, share // 2, rows))
    weights = [back, back_sides[0], *back_far, back_sides[1]]
    first = call(
        near_body,
        [chunks, halves, halves],
        [grads, *grads_sides, *weights],
        at,
        scratch=wide,
        flops=6 * rows * block * outer,
        where=1,
    )
    keep, *gives = call(
        far_body,
        [chunks, halves, halves],
        [*grads_far, *weights, *first],
        at,
        scratch=[pltpu.VMEM((block, rows), bf16), pltpu.VMEM((outer, rows), bf16)],
        flops=2 * rows * block * outer,
        aliases={8: 0, 9: 1, 10: 2},
        where=1,
    )

    middle = []
    for i, give in enumerate(gives):
        sums = over_heads(keep, give, (1,), MIDDLE_FIRST, i)
        middle += call(functools.partial(total_body, i), [struct((share // 2, rows))], [*sums, own])

    arrived = [routed(m, hop(0), (1,)) for m in middle]
    settled = routed(jnp.concatenate(middle), hop(None), (1,))

    parts = [[a] + [routed(a, across_z(k), (0,)) for k in steps] for a in arrived]
    others = [routed(jnp.stack(p), other_core, (0,)) for p in parts]
    grad_ssd, states = call(
        lower_body,
        [struct((inner, rows)), state_shape],
        [*parts[0], *parts[1], *others, out_set, whole_sides[0], *whole_far, whole_sides[1], leading, c_rows, totals],
        at,
        scratch=[pltpu.VMEM((width, rows), bf16)],
        remote=range(15, 18),
        away=(0, 1),
        flops=2 * rows * width * inner,
    )
    held, settled = tie((exchange(states), settled))
    grads = within(grad_ssd, exchange(scanned(held)), MOST)
    keep, give = call(
        whole_body,
        [chunks, chunks],
        [grads, back_set, width_sides[0], *width_far, width_sides[1]],
        at,
        scratch=wide,
        flops=2 * rows * width * outer,
    )
    sums = over_heads(keep, give, (0,), IN_TURN)
    (result,) = call(result_body, [struct((1, rows, share))], [*sums, *arrived, settled], at)
    return result


def solution(mesh):
    placed = (
        P("ctx", None),
        P("section", "heads", "ctx"),
        P("section", "ctx", "heads"),
        P("section", "ctx", "heads"),
        P("section", "ctx", "heads"),
        P("section", "ctx", "heads"),
        P("section", "heads", "ctx"),
        P("section", "heads"),
        P("section", "ctx", "heads", None, None),
    )
    return jax.shard_map(
        local, mesh=mesh, in_specs=placed, out_specs=P("section", "ctx", "heads"), check_vma=False
    )
```

```python
import functools

import jax
import jax.numpy as jnp
from jax import lax
from jax.experimental import pallas as pl
from jax.experimental.pallas import tpu as pltpu
from jax.sharding import PartitionSpec as P

SIDE = 4
CORES = 2
BOTH = (0, 1)
AXES = ("section", "ctx", "heads")
ORDER = (2, 3, 1)
VMEM = 20 * 1024 * 1024
MOST = 54 * 1024 * 1024
bf16, f32 = jnp.bfloat16, jnp.float32


def place(section, x, y, z, core):
    return (((section * SIDE + x) * SIDE + y) * SIDE + z) * CORES + core


def routed(value, move, sections):
    pairs = []
    for section in sections:
        for x in range(SIDE):
            for y in range(SIDE):
                for z in range(SIDE):
                    for core in range(CORES):
                        here = (section, x, y, z, core)
                        pairs.append((place(*here), place(*move(*here))))
    return lax.ppermute(value, AXES, pairs)


def first_half(value, axis):
    return lax.slice_in_dim(value, 0, value.shape[axis] // 2, axis=axis)


def second_half(value, axis):
    return lax.slice_in_dim(value, value.shape[axis] // 2, value.shape[axis], axis=axis)


def sides(value, along, sections):
    return [routed(value, along(k), sections) for k in (1, 3)]


def far(both, along, sections, axis):
    before, after = both
    return [
        routed(first_half(before, axis), along(1), sections),
        routed(second_half(after, axis), along(3), sections),
    ]


def along_x(k):
    return lambda s, x, y, z, c: (s, (x + k) % SIDE, y, z, c)


def along_y(k):
    return lambda s, x, y, z, c: (s, x, (y + k) % SIDE, z, c)


def across_z(k):
    return lambda s, x, y, z, c: (s, x, y, z ^ k, c)


def other_core(s, x, y, z, c):
    return (s, x, y, z, 1 - c)


def hop(to_section):
    return lambda s, x, y, z, c: (s if to_section is None else to_section, x ^ z, y, x, c)


def first_step(k):
    return lambda s, x, y, z, c: (along_y if s == 1 else along_x)(k)(s, x, y, z, c)


def dot(left, right, left_dim, right_dim):
    return lax.dot_general(
        left, right, (((left_dim,), (right_dim,)), ((), ())), preferred_element_type=f32
    )


class Late:
    def __init__(self, source, held, sem):
        self.held, self.copy, self.waited = held, pltpu.make_async_copy(source, held, sem), False
        self.shape = held.shape

    def __getitem__(self, index):
        if not self.waited:
            self.copy.wait()
            self.waited = True
        return self.held[index]


def call(body, outs, args, at=None, scratch=(), flops=0, remote=(), away=(), aliases=(), vmem_limit=VMEM, where=None):
    moved = sum(a.size * a.dtype.itemsize for a in (*args, *outs))
    vmem, hbm = pl.BlockSpec(memory_space=pltpu.VMEM), pl.BlockSpec(memory_space=pltpu.HBM)
    own = [pltpu.VMEM(args[i].shape, args[i].dtype) for i in remote]
    own += [pltpu.VMEM(outs[i].shape, outs[i].dtype) for i in away]

    def run(refs):
        refs = list(refs)
        first = refs[:1] if at is not None else []
        refs = refs[len(first) :]
        ins, results = refs[: len(args)], refs[len(args) : len(args) + len(outs)]
        held = refs[len(args) + len(outs) :]
        sems = held.pop() if own else None
        held, extra = held[: len(own)], held[len(own) :]
        late = []
        for n, i in enumerate(remote):
            late.append(Late(ins[i], held[n], sems.at[n]))
            late[-1].copy.start()
            ins[i] = late[-1]
        targets = list(results)
        for n, i in enumerate(away):
            results[i] = held[len(remote) + n]
        body(*first, *ins, *results, *extra)
        for operand in late:
            if not operand.waited:
                operand[...]
        copies = [
            pltpu.make_async_copy(results[i], targets[i], sems.at[len(remote) + n])
            for n, i in enumerate(away)
        ]
        for copy in copies:
            copy.start()
        for copy in copies:
            copy.wait()

    def kernel(*refs):
        if where is None:
            run(refs)
        else:
            pl.when(refs[0][refs[0].shape[0] - 1] == where)(lambda: run(refs))

    return pl.pallas_call(
        kernel,
        in_specs=[pl.BlockSpec(memory_space=pltpu.SMEM)] * (at is not None)
        + [hbm if i in remote else vmem for i in range(len(args))],
        out_specs=[hbm if i in away else vmem for i in range(len(outs))],
        out_shape=list(outs),
        input_output_aliases=dict(aliases),
        scratch_shapes=own + list(scratch) + ([pltpu.SemaphoreType.DMA((len(own),))] if own else []),
        compiler_params=pltpu.CompilerParams(vmem_limit_bytes=vmem_limit),
        cost_estimate=pl.CostEstimate(flops=flops, bytes_accessed=moved, transcendentals=0),
    )(*([at] if at is not None else []), *args)


def struct(shape, dtype=bf16):
    return jax.ShapeDtypeStruct(shape, dtype)


def behind(index, k):
    return lax.rem(index + SIDE - k, SIDE)


def span(index, size):
    return pl.ds(pl.multiple_of(index * size, size), size)


def tables_body(
    decay, bc_rows, x_rows, state,
    kernel, mixed, x_heads, x_trailing, entry, leading, trailing, totals, b_cols, c_cols, c_rows,
):
    count, length = decay.shape
    size = b_cols.shape[0]
    each = x_heads.shape[0] // count
    exact = lax.Precision.HIGHEST
    earlier = lax.broadcasted_iota(jnp.int32, (length, length), 0)
    later = lax.broadcasted_iota(jnp.int32, (length, length), 1)
    lower = earlier >= later
    inner = (((1,), (0,)), ((), ()))
    last = (((1,), (1,)), ((), ()))
    rates = decay[...]
    sums = lax.dot_general(
        rates, (earlier <= later).astype(f32), inner, precision=exact, preferred_element_type=f32
    )
    columns = lax.dot_general(
        lower.astype(f32), rates, last, precision=exact, preferred_element_type=f32
    )
    b_part, c_part = bc_rows[:, :size], bc_rows[:, size:]
    common = dot(c_part, b_part, 1, 1)
    b_cols[...] = b_part.astype(f32).T.astype(bf16)
    c_cols[...] = c_part.astype(f32).T.astype(bf16)
    c_rows[...] = c_part
    lead = jnp.exp(sums)
    trail = jnp.exp(sums[:, length - 1 :] - sums)
    leading[...] = lead
    trailing[...] = trail
    first = lax.broadcasted_iota(jnp.int32, totals.shape[1:], 0) == 0
    for head in range(count):
        spread = columns[:, head : head + 1] - sums[head : head + 1, :]
        weights = jnp.where(lower, jnp.exp(jnp.minimum(spread, 0.0)), 0.0)
        kernel[head] = weights.astype(bf16)
        mixed[head] = (weights * common).astype(bf16)
        total = jnp.broadcast_to(lead[head : head + 1, length - 1 :], totals.shape[1:])
        high = total.astype(bf16).astype(f32)
        totals[head] = jnp.where(first, high, total - high).astype(bf16)
    for pair in range(count // 2):
        both = slice(pair * 2 * each, (pair + 1) * 2 * each)
        x_pair = x_rows[:, both].astype(f32).T
        x_heads[both, :] = x_pair.astype(bf16)
        for i in range(2):
            head = 2 * pair + i
            own = slice(head * each, (head + 1) * each)
            x_trailing[own, :] = (
                x_pair[i * each : (i + 1) * each, :] * trail[head : head + 1, :]
            ).astype(bf16)
        flat = jnp.concatenate([state[2 * pair], state[2 * pair + 1]], axis=0)
        entry[:, both] = flat.T.astype(bf16)


def rows_body(at, own, u1, u2, v2, u3, w1, wl, wh, w3, w0, o0, o1, o2, o3, piece, u):
    x, y, z, core = at[0], at[1], at[2], at[3]
    fine = w1.shape[1]
    half = u2.shape[0]
    u[0] = own[...]
    u[1] = u1[...]
    u[2, span(core, half), :] = u2[...]
    u[2, span(1 - core, half), :] = v2[...]
    u[3] = u3[...]
    piece[...] = u[behind(x, x ^ z), :, span(core, piece.shape[0])].astype(f32).T.astype(bf16)
    for k, out in enumerate((o0, o1, o2, o3)):
        total = None
        for j, w in enumerate((w0, w1, None, w3)):
            columns = u[k, :, span(behind(y, j), fine)]
            if w is None:
                term = jnp.concatenate([dot(wl[...], columns, 1, 1), dot(wh[...], columns, 1, 1)], axis=0)
            else:
                term = dot(w[...], columns, 1, 1)
            total = term if total is None else total + term
        out[...] = total.astype(bf16)


def entering(grad, leading, c_rows, totals, states):
    count = totals.shape[0]
    each = grad.shape[0] // count
    wide = grad.astype(f32)
    scaled = [
        (wide[h * each : (h + 1) * each] * leading[h : h + 1, :]).astype(bf16) for h in range(count)
    ]
    summed = dot(jnp.concatenate(scaled, axis=0), c_rows[...], 1, 0).astype(bf16)
    for h in range(count):
        states[h, :each, :] = summed[h * each : (h + 1) * each]
        states[h, each:, :] = totals[h]


def sum_body(own, r1, r2, r3, leading, c_rows, totals, grad, states):
    total = own[...].astype(f32)
    for r in (r1, r2, r3):
        total = total + r[...].astype(f32)
    rounded = total.astype(bf16)
    grad[...] = rounded
    entering(rounded, leading, c_rows, totals, states)


def lower_body(
    at, a0, a1, a2, a3, b0, b1, b2, b3, other_a, other_b, w0, w1, wl, wh, w3, leading, c_rows, totals, grad, states, u
):
    x, y, z, core = at[0], at[1], at[2], at[3]
    fine = a0.shape[0]
    for q in range(SIDE):
        base = (z ^ q) * CORES
        for i, (parts, other) in enumerate((((a0, a1, a2, a3), other_a), ((b0, b1, b2, b3), other_b))):
            u[span((base + core) * 2 + i, fine), :] = parts[q][...]
            u[span((base + 1 - core) * 2 + i, fine), :] = other[q]
    total = None
    for k in range(SIDE):
        for j in range(SIDE):
            w = (w0, w1, wl if j < CORES else wh, w3)[k][j % CORES if k == 2 else j]
            rows = u[span(behind(x, j) * SIDE + behind(y, k), fine), :]
            term = dot(w, rows, 1, 0)
            total = term if total is None else total + term
    rounded = total.astype(bf16)
    grad[...] = rounded
    entering(rounded, leading, c_rows, totals, states)


def scan_body(states, exits):
    count, size, _ = exits.shape
    held = jnp.zeros(exits.shape[1:], f32)
    for k in range(count - 1, -1, -1):
        exits[k] = held.astype(bf16)
        total = states[k, size : size + 16, :].astype(f32)
        held = (total[0:1] + total[1:2]) * held + states[k, :size, :].astype(f32)


def block_body(
    grad, leading, entry, leaving, b_cols, x_heads, kernel, mixed, gain, trailing, x_trailing, c_cols, out
):
    count = leading.shape[0]
    inner = grad.shape[0]
    each = inner // count
    size = b_cols.shape[0]
    scaled = []
    for h in range(count):
        own = slice(h * each, (h + 1) * each)
        scaled.append((grad[own, :].astype(f32) * leading[h : h + 1, :]).astype(bf16))
    grad_c = dot(entry[...], jnp.concatenate(scaled, axis=0), 1, 0)
    gained = dot(leaving[...], b_cols[...], 1, 0)
    weighted = None
    for h in range(count):
        own = slice(h * each, (h + 1) * each)
        g = grad[own, :]
        term = kernel[h].astype(f32) * dot(g, x_heads[own, :], 0, 0)
        weighted = term if weighted is None else weighted + term
        inside = dot(g, mixed[h], 1, 0) + gain[h : h + 1, :] * g.astype(f32)
        out[own, :] = (inside + trailing[h : h + 1, :] * gained[own, :]).astype(bf16)
    rounded = weighted.astype(bf16)
    grad_b = dot(c_cols[...], rounded, 1, 0) + dot(leaving[...], x_trailing[...], 0, 0)
    out[inner : inner + size, :] = grad_b.astype(bf16)
    out[inner + size :, :] = (grad_c + dot(b_cols[...], rounded, 1, 1)).astype(bf16)


def to_halves(u, q, core, keep, gives):
    share = keep.shape[1]
    keep[q] = u[span(core, share), :]
    part = share // len(gives)
    for i, give in enumerate(gives):
        give[q] = u[span((1 - core) * len(gives) + i, part), :]


def block_terms(at, g, weights, u):
    for j, w in enumerate(weights):
        rows = span(behind(at[1], j), u.shape[0] // SIDE)
        term = [dot(part[...], g[...], 1, 0) for part in w]
        u[rows, :] = jnp.concatenate(term, axis=0).astype(bf16)


def near_body(at, g0, g1, g3, w0, w1, wl, wh, w3, keep, give_a, give_b, u):
    x, z, core = at[0], at[2], at[3]
    for k, g in ((0, g0), (1, g1), (3, g3)):
        block_terms(at, g, ((w0,), (w1,), (wl, wh), (w3,)), u.at[k])
        to_halves(u.at[k], z ^ x ^ behind(x, k), core, keep, (give_a, give_b))


def far_body(at, gl, gh, w0, w1, wl, wh, w3, k0, k1, k2, keep, give_a, give_b, u, g):
    x, z, core = at[0], at[2], at[3]
    g[: gl.shape[0], :] = gl[...]
    g[gl.shape[0] :, :] = gh[...]
    block_terms(at, g, ((w0,), (w1,), (wl, wh), (w3,)), u)
    to_halves(u, z ^ x ^ behind(x, 2), core, keep, (give_a, give_b))


def whole_body(kept, at, g, w0, w1, wl, wh, w3, out):
    x, y, z, core = at[0], at[1], at[2], at[3]
    side = core if kept else 1 - core
    fine = w0.shape[1]
    for k in range(SIDE):
        q = z ^ behind(x, k)
        for i in range(CORES):
            j = behind(y, side * CORES + i)
            rows = slice(i * fine, (i + 1) * fine)
            if k == 2:
                within = lax.rem(j, CORES)
                w = jnp.where(j < CORES, wl[within], wh[within])
            else:
                w = (w0, w1, None, w3)[k][j]
            out[q, rows, :] = dot(w, g[...], 1, 0).astype(bf16)


def rows_of(keep, q, got, part):
    size = got.shape[1]
    return keep[q, part * size : (part + 1) * size, :].astype(f32) + got[q].astype(f32)


def pair_body(part, keep, got, s1, s2, s3):
    for q, out in zip(ORDER, (s1, s2, s3)):
        out[...] = rows_of(keep, q, got, part).astype(bf16)


def total_of(part, keep, got, received, upstream):
    total = rows_of(keep, 0, got, part)
    for r in received:
        total = total + r[...].astype(f32)
    return total + upstream.astype(f32)


def total_body(part, keep, got, r1, r2, r3, upstream, out):
    size = out.shape[0]
    own = upstream[part * size : (part + 1) * size, :]
    out[...] = total_of(part, keep, got, (r1, r2, r3), own).astype(bf16)


def result_body(at, keep, got, r1, r2, r3, upper, lower, settled, out):
    upstream = jnp.concatenate([upper[...], lower[...]], axis=0)
    total = total_of(0, keep, got, (r1, r2, r3), upstream).astype(bf16).astype(f32)
    chosen = jnp.where(at[4] == 1, settled[...].astype(f32), total)
    out[0] = chosen.T.astype(bf16)


def local(grad_out, w_out, w_in, w_bc, x_act, bc_act, decay, skip_gain, state_in):
    tie = lax.optimization_barrier
    section = lax.axis_index("section")
    ctx = lax.axis_index("ctx")
    heads_at = lax.axis_index("heads")
    x, y = ctx // SIDE, ctx % SIDE
    z, core = heads_at // CORES, heads_at % CORES
    at = jnp.stack([x, y, z, core, section]).astype(jnp.int32)
    rows, width = grad_out.shape
    block = width // SIDE
    share = block // CORES
    half = rows // CORES
    head_count, head_size, state_size = state_in.shape[2:]
    inner = head_count * head_size
    outer = inner + 2 * state_size
    pad = 16
    steps = (1, 2, 3)

    out_sides = sides(w_out[0], first_step, BOTH)
    out_far = far(out_sides, first_step, BOTH, 0)
    pieces = []
    for k in range(SIDE):
        low, count = (half * core, half) if k == 2 else (0, rows)
        pieces.append(lax.dynamic_slice(grad_out, (low, block * ((x + k) % SIDE)), (count, block)))
    own, *pieces = pieces
    pieces = tie(pieces)
    before, across, after = [routed(p, along_x(k), (1,)) for k, p in zip(steps, pieces)]
    upstream = [own, before, across, routed(across, other_core, (1,)), after]

    back = jnp.concatenate([w_in[0], w_bc[0]], axis=1)
    out_far, back = tie((out_far, back))
    back_sides = sides(back, along_y, BOTH)

    (
        kernel, mixed, x_heads, x_trailing, entry, leading, trailing, totals, b_cols, c_cols, c_rows
    ) = call(
        tables_body,
        [
            struct((head_count, rows, rows)), struct((head_count, rows, rows)),
            struct((inner, rows)), struct((inner, rows)), struct((state_size, inner)),
            struct((head_count, rows), f32), struct((head_count, rows), f32),
            struct((head_count, pad, state_size)), struct((state_size, rows)),
            struct((state_size, rows)), struct((rows, state_size)),
        ],
        [decay[0], bc_act[0], x_act[0], state_in[0, 0]],
        remote=range(4),
        flops=2 * rows * rows * inner,
    )
    gain = jnp.broadcast_to(skip_gain[0][:, None], (head_count, rows))
    out_sides, out_far, leading, gain = tie((out_sides, out_far, leading, gain))

    state_shape = struct((head_count, head_size + pad, state_size))

    def exchange(states):
        return lax.all_to_all(states, "ctx", 0, 0)

    def scanned(arrived):
        (exits,) = call(
            scan_body, [struct((head_count, head_size, state_size))], [arrived], away=(0,)
        )
        return exits

    def within(grad_ssd, leaving, vmem_limit=VMEM):
        (grads,) = call(
            block_body,
            [struct((outer, rows))],
            [
                grad_ssd, leading, entry, leaving.reshape(inner, state_size), b_cols, x_heads, kernel, mixed,
                gain, trailing, x_trailing, c_cols,
            ],
            flops=4 * rows * rows * inner,
            remote=range(12),
            vmem_limit=vmem_limit,
        )
        return grads

    chunk = struct((share, rows))
    chunks = struct((SIDE, share, rows))

    def over_heads(keep, give, sections, part=0):
        got = routed(give, other_core, sections)
        sent = call(functools.partial(pair_body, part), [struct(give.shape[1:])] * 3, [keep, got])
        return [keep, got] + [routed(s, across_z(k), sections) for k, s in zip(ORDER, sent)]

    *partial, own = call(
        rows_body,
        [struct((inner, rows))] * SIDE + [chunk],
        [*upstream, out_sides[0], *out_far, out_sides[1], w_out[0]],
        at,
        remote=(9,),
        scratch=[pltpu.VMEM((SIDE, rows, block), bf16)],
        flops=2 * SIDE * rows * block * inner,
        where=1,
    )
    partial, out_sides, out_far = tie((partial, out_sides, out_far))
    received = [routed(partial[k], along_x(-k), (1,)) for k in steps]
    back_far = far(back_sides, along_y, BOTH, 0)
    out_set = jnp.concatenate([w_out[0], out_sides[0], *out_far, out_sides[1]]).reshape(SIDE, inner, -1)
    back_far, out_set = tie((back_far, out_set))
    whole_sides = sides(out_set, along_y, (0,))
    received, back_far = tie((received, back_far))
    back_set = jnp.concatenate([back, back_sides[0], *back_far, back_sides[1]]).reshape(SIDE, -1, outer)
    grad_ssd, states = call(
        sum_body,
        [struct((inner, rows)), state_shape],
        [partial[0], *received, leading, c_rows, totals],
        remote=(4, 5, 6),
        away=(0, 1),
        flops=2 * rows * inner * state_size,
    )

    states, back_set = tie((states, back_set))
    arrived = exchange(states)
    width_sides = sides(back_set, along_x, (0,))
    arrived, whole_sides, width_sides = tie((arrived, whole_sides, width_sides))
    exits = scanned(arrived)
    exits, whole_sides, width_sides = tie((exits, whole_sides, width_sides))
    leaving = exchange(exits)
    whole_far = far(whole_sides, along_y, (0,), 0)
    width_far = far(width_sides, along_x, (0,), 0)
    leaving, whole_far, width_far = tie((leaving, whole_far, width_far))
    grads = within(grad_ssd, leaving)

    grads_sides = sides(grads, along_x, (1,))
    grads_far = far(grads_sides, along_x, (1,), 0)
    wide = [pltpu.VMEM((SIDE, block, rows), bf16)]
    halves = struct((SIDE, share // 2, rows))
    weights = [back, back_sides[0], *back_far, back_sides[1]]
    first = call(
        near_body,
        [chunks, halves, halves],
        [grads, *grads_sides, *weights],
        at,
        scratch=wide,
        flops=6 * rows * block * outer,
        where=1,
    )
    keep, *gives = call(
        far_body,
        [chunks, halves, halves],
        [*grads_far, *weights, *first],
        at,
        scratch=[pltpu.VMEM((block, rows), bf16), pltpu.VMEM((outer, rows), bf16)],
        flops=2 * rows * block * outer,
        aliases={8: 0, 9: 1, 10: 2},
        where=1,
    )

    middle = []
    for i, give in enumerate(gives):
        sums = over_heads(keep, give, (1,), i)
        middle += call(functools.partial(total_body, i), [struct((share // 2, rows))], [*sums, own])

    arrived = [routed(m, hop(0), (1,)) for m in middle]
    settled = routed(jnp.concatenate(middle), hop(None), (1,))

    parts = [[a] + [routed(a, across_z(k), (0,)) for k in steps] for a in arrived]
    others = [routed(jnp.stack(p), other_core, (0,)) for p in parts]
    grad_ssd, states = call(
        lower_body,
        [struct((inner, rows)), state_shape],
        [*parts[0], *parts[1], *others, out_set, whole_sides[0], *whole_far, whole_sides[1], leading, c_rows, totals],
        at,
        scratch=[pltpu.VMEM((width, rows), bf16)],
        remote=range(15, 18),
        away=(0, 1),
        flops=2 * rows * width * inner,
    )
    held, settled = tie((exchange(states), settled))
    grads = within(grad_ssd, exchange(scanned(held)), MOST)
    give, keep = [
        call(
            functools.partial(whole_body, kept),
            [chunks],
            [grads, back_set, width_sides[0], *width_far, width_sides[1]],
            at,
            flops=rows * width * outer,
        )[0]
        for kept in (False, True)
    ]
    sums = over_heads(keep, give, (0,))
    (result,) = call(result_body, [struct((1, rows, share))], [*sums, *arrived, settled], at)
    return result


def solution(mesh):
    placed = (
        P("ctx", None),
        P("section", "heads", "ctx"),
        P("section", "ctx", "heads"),
        P("section", "ctx", "heads"),
        P("section", "ctx", "heads"),
        P("section", "ctx", "heads"),
        P("section", "heads", "ctx"),
        P("section", "heads"),
        P("section", "ctx", "heads", None, None),
    )
    return jax.shard_map(
        local, mesh=mesh, in_specs=placed, out_specs=P("section", "ctx", "heads"), check_vma=False
    )
```
